32 devices in a mesh: sy: 4 (over z), sx: 8 (over y, x, core).
Axes of the slice: x: 2, y: 2, z: 4, core: 2. Of those that a mesh axis runs over, the one named last changes fastest.
Arguments:
- sky_image: float32 [1024, 1024], P('sy', 'sx'), may hold values from -6 to 6
- observed: float32 [1024, 1024], P('sy', 'sx'), may hold values from -6 to 6
- noise_weight: float32 [1024, 1024], P('sy', 'sx'), may hold values from 0.25 to 4
- basis_tiles: bfloat16 [128, 128, 128], P(('sy', 'sx')), may hold values from -3 to 3
- intersection: int32 [8, 8, 4], replicated, may hold values from 0 to 127, as said below
- counts: int32 [8, 8], P('sy', 'sx'), may hold values from 1 to 4
- transfer: float32 [4, 2, 1024, 1024], P(None, None, ('sy', 'sx')), may hold values from -6 to 6
Outputs:
- residual: float32 [1024, 1024], P('sy', 'sx')
- gradient: float32 [1024, 1024], P('sy', 'sx')
The draws below stay inside these ranges and needn't reach their ends.
Inputs may be any that keep to these rules, and one draw needn't show every extreme that they name: `intersection`: every entry names a basis tile held by a device with the same sy index as the sky tile. Of the 8 entries of one device's sky tiles, at most 2 name tiles held by any one device, and in every draw each device reaches 2 at one holder.
All inputs are finite; a program needn't handle non-finite values.
Results may differ from the reference program's by a relative error of at most 0.00045.
Values may be sent and summed in bfloat16 or wider, within the bound.
A program may use at most 128 MiB of HBM per device.

```python
import math
import jax
import jax.numpy as jnp

K = 4
TILE = 128
ROWS_DEV = 256
COLS_DEV = 128
POOL_DEV = 4
NY = 1024
NX = 1024
TILES_Y = 8
TILES_X = 8
POOL = 128


def draw_intersection(key, part):
    tiles_down = ROWS_DEV // TILE
    tiles_across = COLS_DEV // TILE
    band_size = TILES_X // tiles_across
    groups_down = TILES_Y // tiles_down
    tile_row = jnp.arange(TILES_Y, dtype=jnp.int32)[:, None, None]
    tile_column = jnp.arange(TILES_X, dtype=jnp.int32)[None, :, None]
    component = jnp.arange(K, dtype=jnp.int32)[None, None, :]
    position = (tile_row % tiles_down * tiles_across + tile_column % tiles_across) * K + component
    shifts = jax.random.randint(jax.random.fold_in(key, 11), (groups_down, band_size), 0, band_size, dtype=jnp.int32)
    shift_here = shifts[tile_row // tiles_down, tile_column // tiles_across]
    holder = (jnp.maximum(position, 1) + shift_here) % band_size
    local_tile = jax.random.randint(jax.random.fold_in(key, 12), (TILES_Y, TILES_X, K), 0, POOL_DEV, dtype=jnp.int32)
    return (tile_row // tiles_down * band_size + holder) * POOL_DEV + local_tile


def place_ends(drawn, rng, least, top_value):
    extent = drawn.shape
    spot = [jax.random.randint(jax.random.fold_in(rng, axis), (), 0, extent[axis]) for axis in range(len(extent))]
    drawn = drawn.at[tuple(spot)].set(least)
    longest = extent.index(max(extent))
    spot[longest] = (spot[longest] + 1) % extent[longest]
    return drawn.at[tuple(spot)].set(top_value)


def block_scale(stream_key, dims, shards, low, high):
    loudness, own = 1.0, jax.random.fold_in(stream_key, 6)
    for dim, parts in shards:
        heights = jnp.exp(jax.random.uniform(jax.random.fold_in(own, dim), (parts,), jnp.float32, low / len(shards), high / len(shards)))
        loudness = loudness * jnp.repeat(heights, dims[dim] // parts).reshape([-1 if axis == dim else 1 for axis in range(len(dims))])
    return loudness


def normal_values(own_key, extent, scale, reach, pieces=(), kind=jnp.bfloat16):
    entries = jax.random.normal(own_key, extent, jnp.float32) * scale
    if len(pieces) > 0:
        entries = block_scale(own_key, extent, pieces, -0.22, 0.18) * entries
    return jnp.clip(entries, min=-reach, max=reach).astype(kind)


def setup_inputs(seed: int = 0) -> dict:
    arg_keys = jax.random.split(jax.random.key(seed), 8)
    return {
        "sky_image": normal_values(arg_keys[0], (NY, NX), 1.0, 6.0, ((0, 4), (1, 8)), jnp.float32),
        "observed": normal_values(arg_keys[1], (NY, NX), 1.0, 6.0, ((0, 4), (1, 8)), jnp.float32),
        "noise_weight": jnp.clip(jnp.exp(math.log(4.0) - 2.7725887 * jax.random.uniform(arg_keys[2], (NY, NX), jnp.float32) ** block_scale(arg_keys[2], (NY, NX), ((0, 4), (1, 8)), -0.2, 0.2)), 0.25, 4.0),
        "basis_tiles": normal_values(arg_keys[3], (POOL, TILE, TILE), 0.5, 3.0, ((0, 32),)),
        "intersection": draw_intersection(jax.random.fold_in(arg_keys[7], 71), 0),
        "counts": place_ends(jax.random.randint(arg_keys[5], (TILES_Y, TILES_X), 1, K + 1), jax.random.fold_in(arg_keys[5], 1), 1, K).astype(jnp.int32),
        "transfer": normal_values(arg_keys[6], (K, 2, NY, NX), 1.0, 6.0, ((2, 32),), jnp.float32),
    }


tv_weight = 0.5
smoothing = 0.25

def coefficient_maps(basis_tiles, intersection, counts):
    collected = []
    for component in range(K):
        picked = basis_tiles[intersection[:, :, component]].astype(jnp.float32)
        in_use = (counts > component).astype(jnp.float32)
        picked = picked * in_use[:, :, None, None]
        collected.append(picked.transpose(0, 2, 1, 3).reshape(NY, NX))
    return collected

def total_variation(field):
    step_x = jnp.roll(field, -1, axis=1) - field
    step_y = jnp.roll(field, -1, axis=0) - field
    magnitude = jnp.sqrt(step_x * step_x + step_y * step_y + smoothing)
    flow_x = step_x / magnitude
    flow_y = step_y / magnitude
    spread = flow_x - jnp.roll(flow_x, 1, axis=1) + flow_y - jnp.roll(flow_y, 1, axis=0)
    return -spread

def reference(sky_image, observed, noise_weight, basis_tiles, intersection, counts, transfer):
    coef_maps = coefficient_maps(basis_tiles, intersection, counts)
    shuffled = transfer.reshape(K, 2, NY // 128, 128, NX // 128, 128)
    shuffled = shuffled.transpose(0, 1, 3, 2, 5, 4).reshape(K, 2, NY, NX)
    model_sum = 0.0
    for component in range(K):
        response = shuffled[component, 0] + 1j * shuffled[component, 1]
        model_sum = model_sum + jnp.fft.fft2(coef_maps[component] * sky_image) * response
    blurred = jnp.real(jnp.fft.ifft2(model_sum))
    residual = noise_weight * (blurred - observed)
    back_spectrum = jnp.fft.fft2(residual)
    data_grad = 0.0
    for component in range(K):
        response = shuffled[component, 0] + 1j * shuffled[component, 1]
        pulled = jnp.real(jnp.fft.ifft2(back_spectrum * jnp.conj(response)))
        data_grad = data_grad + coef_maps[component] * pulled
    gradient = data_grad + tv_weight * total_variation(sky_image)
    return (residual, gradient)
```

```python
import jax
import jax.numpy as jnp
import numpy as np
from jax import lax
from jax.sharding import PartitionSpec as P

radix = 128
highest = lax.Precision.HIGHEST
tv_weight = 0.5
smoothing = 0.25


def with_halo(block, sides, width):
    for axis, dim in sides:
        count = lax.axis_size(axis)
        forward = [(i, i + 1) for i in range(count - 1)]
        forward.append((count - 1, 0))
        backward = [(target, source) for source, target in forward]
        low = lax.ppermute(
            lax.slice_in_dim(block, block.shape[dim] - width, None, axis=dim), axis, forward
        )
        high = lax.ppermute(lax.slice_in_dim(block, 0, width, axis=dim), axis, backward)
        block = jnp.concatenate([low, block, high], axis=dim)
    return block


def circle(left_index, right_index, length, orient):
    product = left_index[:, None] * right_index[None, :] % length
    angles = product.astype(jnp.float32) * (2.0 * jnp.pi / length)
    return (jnp.cos(angles), orient * jnp.sin(angles))


def contract(pattern, operand, matrix):
    return jnp.einsum(pattern, operand, matrix, precision=highest)


def forward_last(stacked):
    num_parts, num_fields, num_lines, length = stacked.shape
    short_size = length // radix
    pieces = stacked.reshape(num_parts, num_fields, num_lines, short_size, radix)
    short_index = jnp.arange(short_size, dtype=jnp.int32)
    long_index = jnp.arange(radix, dtype=jnp.int32)
    cos_short, sin_short = circle(short_index, short_index, short_size, -1.0)
    cos_turn, sin_turn = circle(short_index, long_index, length, -1.0)
    cos_long, sin_long = circle(long_index, long_index, radix, -1.0)
    first_form = "fmba,bk->fmka"
    real_part = contract(first_form, pieces[0], cos_short)
    imag_part = contract(first_form, pieces[0], sin_short)
    if num_parts == 2:
        real_part = real_part - contract(first_form, pieces[1], sin_short)
        imag_part = imag_part + contract(first_form, pieces[1], cos_short)
    turned_real = real_part * cos_turn - imag_part * sin_turn
    turned_imag = real_part * sin_turn + imag_part * cos_turn
    second_form = "fmka,aj->fmkj"
    out_real = contract(second_form, turned_real, cos_long) - contract(
        second_form, turned_imag, sin_long
    )
    out_imag = contract(second_form, turned_real, sin_long) + contract(
        second_form, turned_imag, cos_long
    )
    return jnp.stack([out_real, out_imag]).reshape(2, num_fields, num_lines, length)


def inverse_last(stacked, real_only):
    num_fields, num_lines, length = (stacked.shape[1], stacked.shape[2], stacked.shape[3])
    short_size = length // radix
    pieces = stacked.reshape(2, num_fields, num_lines, short_size, radix)
    short_index = jnp.arange(short_size, dtype=jnp.int32)
    long_index = jnp.arange(radix, dtype=jnp.int32)
    cos_long, sin_long = circle(long_index, long_index, radix, 1.0)
    cos_turn, sin_turn = circle(short_index, long_index, length, 1.0)
    cos_short, sin_short = circle(short_index, short_index, short_size, 1.0)
    first_form = "fmkj,ja->fmka"
    real_part = contract(first_form, pieces[0], cos_long) - contract(
        first_form, pieces[1], sin_long
    )
    imag_part = contract(first_form, pieces[0], sin_long) + contract(
        first_form, pieces[1], cos_long
    )
    turned_real = real_part * cos_turn - imag_part * sin_turn
    turned_imag = real_part * sin_turn + imag_part * cos_turn
    second_form = "fmka,kb->fmba"
    out_real = contract(second_form, turned_real, cos_short) - contract(
        second_form, turned_imag, sin_short
    )
    if real_only:
        return out_real.reshape(1, num_fields, num_lines, length)
    out_imag = contract(second_form, turned_real, sin_short) + contract(
        second_form, turned_imag, cos_short
    )
    return jnp.stack([out_real, out_imag]).reshape(2, num_fields, num_lines, length)


def to_spectra(pixels):
    columns = lax.all_to_all(
        jnp.swapaxes(pixels, 2, 3), "sy", split_axis=2, concat_axis=3, tiled=True
    )
    along_y = forward_last(columns)
    blocks = lax.all_to_all(along_y, "sy", split_axis=3, concat_axis=2, tiled=True)
    lines = lax.all_to_all(
        jnp.swapaxes(blocks, 2, 3), "sx", split_axis=2, concat_axis=3, tiled=True
    )
    return forward_last(lines)


def from_spectra(spectrum, normalizer):
    along_x = inverse_last(spectrum, False)
    blocks = lax.all_to_all(along_x, "sx", split_axis=3, concat_axis=2, tiled=True)
    columns = lax.all_to_all(
        jnp.swapaxes(blocks, 2, 3), "sy", split_axis=2, concat_axis=3, tiled=True
    )
    values = inverse_last(columns, True) * normalizer
    pixel_blocks = lax.all_to_all(values, "sy", split_axis=3, concat_axis=2, tiled=True)
    return jnp.swapaxes(pixel_blocks, 2, 3)[0]


def generic_device(sky_image, observed, noise_weight, basis_tiles, intersection, counts, transfer):
    height, breadth = sky_image.shape
    pool_size, tile_side = (basis_tiles.shape[0], basis_tiles.shape[1])
    components = intersection.shape[2]
    tiles_down = height // tile_side
    tiles_across = breadth // tile_side
    band_size = lax.axis_size("sx")
    sky_row = lax.axis_index("sy")
    sky_column = lax.axis_index("sx")
    num_requests = tiles_down * tiles_across * components
    zero_index = jnp.zeros((), jnp.int32)
    own_lists = lax.dynamic_slice(
        intersection,
        (sky_row * tiles_down, sky_column * tiles_across, zero_index),
        (tiles_down, tiles_across, components),
    ).reshape(num_requests)
    band_start = sky_row * band_size * pool_size
    band_index = own_lists - band_start
    flat_tiles = basis_tiles.reshape(pool_size, tile_side * tile_side)
    piece = lax.all_gather(flat_tiles, "sx", axis=0, tiled=True)
    piece_count = piece.shape[0]
    hits = (band_index[:, None] == jnp.arange(piece_count, dtype=jnp.int32)[None, :]).astype(
        jnp.bfloat16
    )
    coefficient = jnp.dot(hits, piece, preferred_element_type=jnp.float32)
    in_use = (jnp.arange(components, dtype=jnp.int32)[None, None, :] < counts[:, :, None]).astype(
        jnp.float32
    )
    coef_maps = (
        coefficient.reshape(tiles_down, tiles_across, components, tile_side, tile_side)
        * in_use[:, :, :, None, None]
    )
    weights = coef_maps.transpose(2, 0, 3, 1, 4).reshape(components, height, breadth)
    normalizer = 1.0 / (transfer.shape[2] * lax.axis_size("sy") * band_size * transfer.shape[3])
    spectra = to_spectra((weights * sky_image[None])[None])
    trans_real = transfer[:, 0]
    trans_imag = transfer[:, 1]
    model_real = jnp.sum(spectra[0] * trans_real - spectra[1] * trans_imag, axis=0)
    model_imag = jnp.sum(spectra[0] * trans_imag + spectra[1] * trans_real, axis=0)
    blurred = from_spectra(jnp.stack([model_real, model_imag])[:, None], normalizer)[0]
    residual = noise_weight * (blurred - observed)
    back_spectrum = to_spectra(residual[None, None])
    pull_real = back_spectrum[0] * trans_real + back_spectrum[1] * trans_imag
    pull_imag = back_spectrum[1] * trans_real - back_spectrum[0] * trans_imag
    pulled = from_spectra(jnp.stack([pull_real, pull_imag]), normalizer)
    data_grad = jnp.sum(weights * pulled, axis=0)
    framed = with_halo(sky_image, (("sy", 0), ("sx", 1)), 1)
    step_x = framed[:-1, 1:] - framed[:-1, :-1]
    step_y = framed[1:, :-1] - framed[:-1, :-1]
    magnitude = jnp.sqrt(step_x * step_x + step_y * step_y + smoothing)
    flow_x = step_x / magnitude
    flow_y = step_y / magnitude
    spread = flow_x[1:, 1:] - flow_x[1:, :-1] + flow_y[1:, 1:] - flow_y[:-1, 1:]
    gradient = data_grad - tv_weight * spread
    return (residual, gradient)


largest_dense = 1024


def dense_tables(height, breadth, bands, band_size):
    count = bands * band_size
    columns = breadth // count
    spot = np.arange(breadth)
    owner, column = (spot // columns, spot % columns)
    pixel = (owner % band_size) * columns * bands + (owner // band_size) * columns + column
    def frequency(length):
        step = np.arange(length)
        return (length // radix) * (step % radix) + step // radix
    def table(left, right, length):
        angle = (left[:, None] * right[None, :] % length) * (2.0 * np.pi / length)
        return np.cos(angle).astype(np.float32), np.sin(angle).astype(np.float32)
    return (
        table(frequency(height), np.arange(height), height),
        table(pixel, frequency(breadth), breadth),
    )


def exchange(blocks):
    return lax.all_to_all(blocks, ("sy", "sx"), split_axis=0, concat_axis=0)


def product(pattern, left, right):
    return jnp.einsum(pattern, left, right, precision=lax.Precision.HIGH)


def total_variation(sky_image):
    framed = with_halo(sky_image, (("sy", 0), ("sx", 1)), 1)
    step_x = framed[:-1, 1:] - framed[:-1, :-1]
    step_y = framed[1:, :-1] - framed[:-1, :-1]
    magnitude = jnp.sqrt(step_x * step_x + step_y * step_y + smoothing)
    flow_x = step_x / magnitude
    flow_y = step_y / magnitude
    return flow_x[1:, 1:] - flow_x[1:, :-1] + flow_y[1:, 1:] - flow_y[:-1, 1:]


def on_device(sky_image, observed, noise_weight, basis_tiles, intersection, counts, transfer):
    rows, side = sky_image.shape
    bands, band_size = (lax.axis_size("sy"), lax.axis_size("sx"))
    devices = bands * band_size
    height, breadth = (rows * bands, side * band_size)
    if max(height, breadth) > largest_dense:
        return generic_device(
            sky_image, observed, noise_weight, basis_tiles, intersection, counts, transfer
        )
    columns = breadth // devices
    lines = height // devices
    pool = basis_tiles.shape[0]
    tile_side = basis_tiles.shape[1]
    components = intersection.shape[2]
    tiles_down = rows // tile_side
    tiles_across = side // tile_side
    entries = tiles_down * tiles_across * components
    my_band, my_column = (lax.axis_index("sy"), lax.axis_index("sx"))
    (cos_y, sin_y), (cos_x, sin_x) = dense_tables(height, breadth, bands, band_size)

    lists = intersection.reshape(bands, tiles_down, band_size, tiles_across, components)
    lists = lists.transpose(0, 2, 1, 3, 4).reshape(bands, band_size, entries)
    slots = jnp.arange(2, dtype=jnp.int32)
    asked = lax.dynamic_index_in_dim(lists, my_band, 0, False)
    local = asked - (my_band * band_size + my_column) * pool
    hit = (local >= 0) & (local < pool)
    rank = jnp.cumsum(hit.astype(jnp.int32), axis=1) - 1
    chosen = (
        (hit & (rank == slots[:, None, None]))[..., None]
        & (local[None, ..., None] == jnp.arange(pool, dtype=jnp.int32))
    ).any(axis=2)
    sent = jnp.einsum(
        "rdp,pyx->dryx", chosen.astype(jnp.bfloat16), basis_tiles, preferred_element_type=jnp.bfloat16
    )
    sent = sent.reshape(band_size, 2, tile_side, bands, columns).transpose(3, 0, 1, 2, 4)
    tiles = exchange(sent.reshape(devices, 2, tile_side, columns))
    tiles = tiles.reshape(bands, band_size, 2, tile_side, columns)
    wanted = lax.dynamic_index_in_dim(lists, my_column, 1, False)
    holder = wanted // pool - jnp.arange(bands, dtype=jnp.int32)[:, None] * band_size
    holds = holder[..., None] == jnp.arange(band_size, dtype=jnp.int32)
    place = jnp.cumsum(holds.astype(jnp.int32), axis=1) - 1
    pick = holds[..., None] & (place[..., None] == slots)
    all_counts = lax.all_gather(counts, "sy").reshape(bands, tiles_down, tiles_across, 1)
    in_use = (jnp.arange(components, dtype=jnp.int32) < all_counts).reshape(bands, entries)
    pick = (pick & in_use[..., None, None]).astype(jnp.bfloat16)
    weights = jnp.einsum("behr,bhryc->beyc", pick, tiles, preferred_element_type=jnp.float32)
    weights = weights.reshape(bands, tiles_down, components, tile_side, columns)
    weights = weights.transpose(2, 0, 1, 3, 4).reshape(components, height, columns)

    pixels = lax.all_to_all(
        jnp.stack([sky_image, observed, noise_weight]), "sy", split_axis=2, concat_axis=1, tiled=True
    )
    sky, seen, noise = (pixels[0], pixels[1], pixels[2])
    normalizer = 1.0 / (height * breadth)

    def to_lines(real_fields):
        parts = jnp.stack(
            [product("sy,kyc->skc", cos_y, real_fields), -product("sy,kyc->skc", sin_y, real_fields)]
        )
        fields = real_fields.shape[0]
        blocks = parts.reshape(2, devices, lines, fields, columns).transpose(1, 0, 2, 3, 4)
        got = exchange(blocks)
        got = got.transpose(1, 3, 2, 0, 4).reshape(2, fields, lines, breadth)
        real = product("ksx,xt->kst", got[0], cos_x) + product("ksx,xt->kst", got[1], sin_x)
        imag = product("ksx,xt->kst", got[1], cos_x) - product("ksx,xt->kst", got[0], sin_x)
        return real, imag

    def to_columns(real, imag):
        back_real = product("kst,xt->ksx", real, cos_x) - product("kst,xt->ksx", imag, sin_x)
        back_imag = product("kst,xt->ksx", imag, cos_x) + product("kst,xt->ksx", real, sin_x)
        fields = real.shape[0]
        blocks = jnp.stack([back_real, back_imag]).reshape(2, fields, lines, devices, columns)
        got = exchange(blocks.transpose(3, 0, 2, 1, 4))
        got = got.transpose(1, 0, 2, 3, 4).reshape(2, height, fields, columns)
        return (
            product("sy,skc->kyc", cos_y, got[0]) - product("sy,skc->kyc", sin_y, got[1])
        ) * normalizer

    real, imag = to_lines(weights * sky)
    trans_real, trans_imag = (transfer[:, 0], transfer[:, 1])
    model_real = jnp.sum(real * trans_real - imag * trans_imag, axis=0, keepdims=True)
    model_imag = jnp.sum(real * trans_imag + imag * trans_real, axis=0, keepdims=True)
    blurred = to_columns(model_real, model_imag)[0]
    left_over = noise * (blurred - seen)
    real, imag = to_lines(left_over[None])
    pulled = to_columns(real * trans_real + imag * trans_imag, imag * trans_real - real * trans_imag)
    data_grad = jnp.sum(weights * pulled, axis=0)
    outputs = lax.all_to_all(
        jnp.stack([left_over, data_grad]), "sy", split_axis=1, concat_axis=2, tiled=True
    )
    return (outputs[0], outputs[1] - tv_weight * total_variation(sky_image))


def solution(mesh):
    placed = (
        P("sy", "sx"),
        P("sy", "sx"),
        P("sy", "sx"),
        P(("sy", "sx"), None, None),
        P(),
        P("sy", "sx"),
        P(None, None, ("sy", "sx"), None),
    )
    return jax.shard_map(
        on_device,
        mesh=mesh,
        in_specs=placed,
        out_specs=(P("sy", "sx"), P("sy", "sx")),
        check_vma=False,
    )
```

```python
import jax
import jax.numpy as jnp
import numpy as np
from jax import lax
from jax.experimental import pallas as pl
from jax.experimental.pallas import tpu as pltpu
from jax.sharding import PartitionSpec as P

radix = 128
highest = lax.Precision.HIGHEST
tv_weight = 0.5
smoothing = 0.25


def with_halo(block, sides, width):
    for axis, dim in sides:
        count = lax.axis_size(axis)
        forward = [(i, i + 1) for i in range(count - 1)]
        forward.append((count - 1, 0))
        backward = [(target, source) for source, target in forward]
        low = lax.ppermute(
            lax.slice_in_dim(block, block.shape[dim] - width, None, axis=dim), axis, forward
        )
        high = lax.ppermute(lax.slice_in_dim(block, 0, width, axis=dim), axis, backward)
        block = jnp.concatenate([low, block, high], axis=dim)
    return block


def circle(left_index, right_index, length, orient):
    product = left_index[:, None] * right_index[None, :] % length
    angles = product.astype(jnp.float32) * (2.0 * jnp.pi / length)
    return (jnp.cos(angles), orient * jnp.sin(angles))


def contract(pattern, operand, matrix):
    return jnp.einsum(pattern, operand, matrix, precision=highest)


def forward_last(stacked):
    num_parts, num_fields, num_lines, length = stacked.shape
    short_size = length // radix
    pieces = stacked.reshape(num_parts, num_fields, num_lines, short_size, radix)
    short_index = jnp.arange(short_size, dtype=jnp.int32)
    long_index = jnp.arange(radix, dtype=jnp.int32)
    cos_short, sin_short = circle(short_index, short_index, short_size, -1.0)
    cos_turn, sin_turn = circle(short_index, long_index, length, -1.0)
    cos_long, sin_long = circle(long_index, long_index, radix, -1.0)
    first_form = "fmba,bk->fmka"
    real_part = contract(first_form, pieces[0], cos_short)
    imag_part = contract(first_form, pieces[0], sin_short)
    if num_parts == 2:
        real_part = real_part - contract(first_form, pieces[1], sin_short)
        imag_part = imag_part + contract(first_form, pieces[1], cos_short)
    turned_real = real_part * cos_turn - imag_part * sin_turn
    turned_imag = real_part * sin_turn + imag_part * cos_turn
    second_form = "fmka,aj->fmkj"
    out_real = contract(second_form, turned_real, cos_long) - contract(
        second_form, turned_imag, sin_long
    )
    out_imag = contract(second_form, turned_real, sin_long) + contract(
        second_form, turned_imag, cos_long
    )
    return jnp.stack([out_real, out_imag]).reshape(2, num_fields, num_lines, length)


def inverse_last(stacked, real_only):
    num_fields, num_lines, length = (stacked.shape[1], stacked.shape[2], stacked.shape[3])
    short_size = length // radix
    pieces = stacked.reshape(2, num_fields, num_lines, short_size, radix)
    short_index = jnp.arange(short_size, dtype=jnp.int32)
    long_index = jnp.arange(radix, dtype=jnp.int32)
    cos_long, sin_long = circle(long_index, long_index, radix, 1.0)
    cos_turn, sin_turn = circle(short_index, long_index, length, 1.0)
    cos_short, sin_short = circle(short_index, short_index, short_size, 1.0)
    first_form = "fmkj,ja->fmka"
    real_part = contract(first_form, pieces[0], cos_long) - contract(
        first_form, pieces[1], sin_long
    )
    imag_part = contract(first_form, pieces[0], sin_long) + contract(
        first_form, pieces[1], cos_long
    )
    turned_real = real_part * cos_turn - imag_part * sin_turn
    turned_imag = real_part * sin_turn + imag_part * cos_turn
    second_form = "fmka,kb->fmba"
    out_real = contract(second_form, turned_real, cos_short) - contract(
        second_form, turned_imag, sin_short
    )
    if real_only:
        return out_real.reshape(1, num_fields, num_lines, length)
    out_imag = contract(second_form, turned_real, sin_short) + contract(
        second_form, turned_imag, cos_short
    )
    return jnp.stack([out_real, out_imag]).reshape(2, num_fields, num_lines, length)


def to_spectra(pixels):
    columns = lax.all_to_all(
        jnp.swapaxes(pixels, 2, 3), "sy", split_axis=2, concat_axis=3, tiled=True
    )
    along_y = forward_last(columns)
    blocks = lax.all_to_all(along_y, "sy", split_axis=3, concat_axis=2, tiled=True)
    lines = lax.all_to_all(
        jnp.swapaxes(blocks, 2, 3), "sx", split_axis=2, concat_axis=3, tiled=True
    )
    return forward_last(lines)


def from_spectra(spectrum, normalizer):
    along_x = inverse_last(spectrum, False)
    blocks = lax.all_to_all(along_x, "sx", split_axis=3, concat_axis=2, tiled=True)
    columns = lax.all_to_all(
        jnp.swapaxes(blocks, 2, 3), "sy", split_axis=2, concat_axis=3, tiled=True
    )
    values = inverse_last(columns, True) * normalizer
    pixel_blocks = lax.all_to_all(values, "sy", split_axis=3, concat_axis=2, tiled=True)
    return jnp.swapaxes(pixel_blocks, 2, 3)[0]


def generic_device(sky_image, observed, noise_weight, basis_tiles, intersection, counts, transfer):
    height, breadth = sky_image.shape
    pool_size, tile_side = (basis_tiles.shape[0], basis_tiles.shape[1])
    components = intersection.shape[2]
    tiles_down = height // tile_side
    tiles_across = breadth // tile_side
    band_size = lax.axis_size("sx")
    sky_row = lax.axis_index("sy")
    sky_column = lax.axis_index("sx")
    num_requests = tiles_down * tiles_across * components
    zero_index = jnp.zeros((), jnp.int32)
    own_lists = lax.dynamic_slice(
        intersection,
        (sky_row * tiles_down, sky_column * tiles_across, zero_index),
        (tiles_down, tiles_across, components),
    ).reshape(num_requests)
    band_start = sky_row * band_size * pool_size
    band_index = own_lists - band_start
    flat_tiles = basis_tiles.reshape(pool_size, tile_side * tile_side)
    piece = lax.all_gather(flat_tiles, "sx", axis=0, tiled=True)
    piece_count = piece.shape[0]
    hits = (band_index[:, None] == jnp.arange(piece_count, dtype=jnp.int32)[None, :]).astype(
        jnp.bfloat16
    )
    coefficient = jnp.dot(hits, piece, preferred_element_type=jnp.float32)
    in_use = (jnp.arange(components, dtype=jnp.int32)[None, None, :] < counts[:, :, None]).astype(
        jnp.float32
    )
    coef_maps = (
        coefficient.reshape(tiles_down, tiles_across, components, tile_side, tile_side)
        * in_use[:, :, :, None, None]
    )
    weights = coef_maps.transpose(2, 0, 3, 1, 4).reshape(components, height, breadth)
    normalizer = 1.0 / (transfer.shape[2] * lax.axis_size("sy") * band_size * transfer.shape[3])
    spectra = to_spectra((weights * sky_image[None])[None])
    trans_real = transfer[:, 0]
    trans_imag = transfer[:, 1]
    model_real = jnp.sum(spectra[0] * trans_real - spectra[1] * trans_imag, axis=0)
    model_imag = jnp.sum(spectra[0] * trans_imag + spectra[1] * trans_real, axis=0)
    blurred = from_spectra(jnp.stack([model_real, model_imag])[:, None], normalizer)[0]
    residual = noise_weight * (blurred - observed)
    back_spectrum = to_spectra(residual[None, None])
    pull_real = back_spectrum[0] * trans_real + back_spectrum[1] * trans_imag
    pull_imag = back_spectrum[1] * trans_real - back_spectrum[0] * trans_imag
    pulled = from_spectra(jnp.stack([pull_real, pull_imag]), normalizer)
    data_grad = jnp.sum(weights * pulled, axis=0)
    framed = with_halo(sky_image, (("sy", 0), ("sx", 1)), 1)
    step_x = framed[:-1, 1:] - framed[:-1, :-1]
    step_y = framed[1:, :-1] - framed[:-1, :-1]
    magnitude = jnp.sqrt(step_x * step_x + step_y * step_y + smoothing)
    flow_x = step_x / magnitude
    flow_y = step_y / magnitude
    spread = flow_x[1:, 1:] - flow_x[1:, :-1] + flow_y[1:, 1:] - flow_y[:-1, 1:]
    gradient = data_grad - tv_weight * spread
    return (residual, gradient)


lanes = 128
group = 32
num_groups = 4
bands = 4
band_size = 8
devices = 32
size = 1024
MESH = pl.DeviceIdType.MESH


def split_table(values):
    high = values.astype(jnp.bfloat16)
    return high, (values - high.astype(np.float64)).astype(jnp.bfloat16)


def tables():
    spot = np.arange(size)
    owner, column = (spot // group, spot % group)
    pixel = (owner % band_size) * lanes + (owner // band_size) * group + column
    frequency = (size // radix) * (spot % radix) + spot // radix
    angle = (frequency[:, None] * spot[None, :] % size) * (2.0 * np.pi / size)
    parts = np.stack([np.cos(angle), -np.sin(angle)]).reshape(2, devices, group, size)
    along_y = parts.transpose(1, 0, 2, 3).reshape(2 * size, size)
    angle = (pixel[:, None] * frequency[None, :] % size) * (2.0 * np.pi / size)
    cos_high, cos_low = split_table(np.cos(angle))
    sin_high, sin_low = split_table(np.sin(angle))
    return (
        *split_table(along_y),
        cos_high,
        sin_high,
        cos_low,
        sin_low,
        *split_table(np.ascontiguousarray(along_y.T)),
    )


def split(values):
    high = values.astype(jnp.bfloat16)
    return high, (values - high.astype(jnp.float32)).astype(jnp.bfloat16)


def mul(left, right):
    return jnp.dot(left, right, preferred_element_type=jnp.float32)


def mul_t(left, right):
    return lax.dot_general(
        left, right, (((1,), (1,)), ((), ())), preferred_element_type=jnp.float32
    )


def cut(values, index):
    return values[:, index * group : (index + 1) * group]


def lane_groups(rows):
    return lax.broadcasted_iota(jnp.int32, (rows, lanes), 1) // group


def pick_groups(pieces):
    where = lane_groups(pieces[0].shape[0])
    out = pieces[0]
    for index in range(1, num_groups):
        out = jnp.where(where == index, pieces[index], out)
    return out


def fold(values):
    values = values + pltpu.roll(values, 64, 1)
    return values + pltpu.roll(values, 32, 1)


def pull(total, sky, left, right, below, above, below_left, above_right):
    rows = sky.shape[0]
    lane = lax.broadcasted_iota(jnp.int32, sky.shape, 1)
    row = lax.broadcasted_iota(jnp.int32, sky.shape, 0)

    def flows(step_x, step_y):
        magnitude = jnp.sqrt(step_x * step_x + step_y * step_y + smoothing)
        return step_x / magnitude, step_y / magnitude

    next_x = jnp.where(lane == lanes - 1, right, pltpu.roll(sky, lanes - 1, 1))
    next_y = jnp.where(row == rows - 1, below, pltpu.roll(sky, rows - 1, 0))
    flow_x, flow_y = flows(next_x - sky, next_y - sky)
    left_next = jnp.where(row == rows - 1, below_left, pltpu.roll(left, rows - 1, 0))
    side_x, _ = flows(sky - left, left_next - left)
    side_x = side_x[:, 0:1]
    above_next = jnp.where(lane[0:8] == lanes - 1, above_right, pltpu.roll(above, lanes - 1, 1))
    _, top_y = flows(above_next - above, sky[0:1] - above)
    before_x = jnp.where(lane == 0, side_x, pltpu.roll(flow_x, 1, 1))
    before_y = jnp.where(row == 0, top_y[7:8], pltpu.roll(flow_y, 1, 0))
    total[...] = flow_x - before_x + flow_y - before_y


def kernel(
    sky, seen, noise, mask, basis, tile_mult, pick_mult,
    trans_hbm, fyh_hbm, fyl_hbm, cxh_hbm, sxh_hbm, cxl_hbm, sxl_hbm, gh_hbm, gl_hbm,
    res_out, grad_out,
    trans, fyh, fyl, cxh, sxh, cxl, sxl, gh, gl,
    sky_s, sky_r, seen_s, seen_r, noise_s, noise_r, tile_s, tile_r,
    two_s, two_r, three_s, three_r, four_s, four_r, five_s, five_r,
    res_s, res_r, grad_s, grad_r,
    halo_left, halo_right, halo_below, halo_above, halo_bl, halo_ar,
    weights, fields, wide, narrow, tall, spread,
    load_sem, send_sem, recv_sem,
):
    my_y, my_x = (lax.axis_index("sy"), lax.axis_index("sx"))
    me = my_y * band_size + my_x
    barrier = pltpu.get_barrier_semaphore()

    def greet(step, carry):
        other = lax.rem(me + step, devices)
        pl.semaphore_signal(
            barrier, inc=1, device_id=(other // band_size, lax.rem(other, band_size)),
            device_id_type=MESH,
        )
        return carry

    lax.fori_loop(1, devices, greet, 0)
    loads = []
    pairs = (
        (fyh_hbm, fyh), (fyl_hbm, fyl), (cxh_hbm, cxh), (sxh_hbm, sxh), (cxl_hbm, cxl),
        (sxl_hbm, sxl), (trans_hbm, trans), (gh_hbm, gh), (gl_hbm, gl),
    )
    for index, (source, target) in enumerate(pairs):
        loads.append(pltpu.make_async_copy(source, target, load_sem.at[index]))
        loads[-1].start()

    def send(source, target, phase, where):
        pltpu.make_async_remote_copy(
            src_ref=source, dst_ref=target, send_sem=send_sem.at[phase],
            recv_sem=recv_sem.at[phase], device_id=where, device_id_type=MESH,
        ).start()

    def total_of(buffer, phase):
        part = buffer.at[pl.ds(0, buffer.shape[0] - 1)]
        return pltpu.make_async_remote_copy(
            src_ref=part, dst_ref=part, send_sem=send_sem.at[phase],
            recv_sem=recv_sem.at[phase], device_id=(lax.rem(my_y + 1, bands), my_x),
            device_id_type=MESH,
        )

    def to_all(source, target, phase, other):
        @pl.when(other != me)
        def _():
            send(
                source.at[other], target.at[me], phase,
                (other // band_size, lax.rem(other, band_size)),
            )

        @pl.when(other == me)
        def _():
            target[me] = source[me]

    def to_band(source, target, phase, other):
        @pl.when(other != my_y)
        def _():
            send(source.at[other], target.at[my_y], phase, (other, my_x))

        @pl.when(other == my_y)
        def _():
            target[my_y] = source[my_y]

    def pack(block, other):
        return jnp.concatenate(
            [cut(block[g * 64 : (g + 1) * 64], other) for g in range(num_groups)], axis=1
        )

    for other in range(bands):
        sky_s[other, 0:64] = pack(sky[...], other)
        sky_s[other, 64:72] = mask[...]
    pl.semaphore_wait(barrier, devices - 1)
    for other in range(bands):
        to_band(sky_s, sky_r, 0, other)

    for other in range(bands):
        packs = []
        for t in range(4):
            part = cut(basis[t].astype(jnp.float32), other)
            packs.append(
                jnp.concatenate([part[0:64], part[0:64], part[64:128], part[64:128]], axis=1)
            )

        def choose(column, carry):
            acc = tile_mult[column, 0:1] * packs[0]
            for t in range(1, 4):
                acc = acc + tile_mult[column, t : t + 1] * packs[t]
            tile_s[other * band_size + column] = acc.astype(jnp.bfloat16)
            to_all(tile_s, tile_r, 1, other * band_size + column)
            return carry

        lax.fori_loop(0, band_size, choose, 0)

    for other in range(bands):
        seen_s[other] = pack(seen[...], other)
        noise_s[other] = pack(noise[...], other)
        to_band(seen_s, seen_r, 2, other)
        to_band(noise_s, noise_r, 3, other)
    up, down = (lax.rem(my_y + bands - 1, bands), lax.rem(my_y + 1, bands))
    west, east = (lax.rem(my_x + band_size - 1, band_size), lax.rem(my_x + 1, band_size))
    first, last = (sky.at[pl.ds(0, 8)], sky.at[pl.ds(248, 8)])
    halos = (
        (sky_s.at[0, pl.ds(0, 64)], halo_right, (my_y, west)),
        (sky_s.at[bands - 1, pl.ds(0, 64)], halo_left, (my_y, east)),
        (first, halo_below, (up, my_x)),
        (first, halo_bl, (up, east)),
        (last, halo_above, (down, my_x)),
        (last, halo_ar, (down, west)),
    )
    for index, (source, target, where) in enumerate(halos):
        send(source, target, 9 + index, where)

    total_of(sky_r, 0).wait_recv()
    total_of(tile_r, 1).wait_recv()

    def weigh(band, carry):
        parts = []
        for e in range(8):
            acc = None
            for h in range(band_size):
                term = pick_mult[band * 8 + e, h : h + 1] * tile_r[band * band_size + h].astype(
                    jnp.float32
                )
                acc = term if acc is None else acc + term
            acc = (acc + pltpu.roll(acc, 96, 1)) * sky_r[band, 64 + e : 65 + e]
            parts.append(acc)
        for g in range(num_groups):
            down_tile, half = (g // 2, g % 2)
            block = jnp.concatenate(
                [cut(parts[down_tile * 4 + k], 2 * half) for k in range(4)], axis=1
            )
            rows = pl.ds(pl.multiple_of(band * 256 + g * 64, 64), 64)
            weights[rows] = block
            high, low = split(
                block * jnp.concatenate([cut(sky_r[band, 0:64], g)] * num_groups, axis=1)
            )
            fields[rows, 0:128] = high
            fields[rows, 128:256] = low
        return carry

    lax.fori_loop(0, bands, weigh, 0)
    loads[0].wait()
    loads[1].wait()

    def along_y(step):
        part = lax.rem(me // 4 + 1 + step, 8)
        rows = pl.ds(pl.multiple_of(part * 256, 256), 256)
        both = mul(fyh[rows], fields[...])
        return part, both[:, 0:128] + both[:, 128:256] + mul(fyl[rows], fields[:, 0:128])

    def forward_y(step, carry):
        part, out = along_y(step)
        for j in range(4):
            other = part * 4 + j
            two_s[other] = out[j * 64 : (j + 1) * 64]
            to_all(two_s, two_r, 4, other)
        return carry

    lax.fori_loop(0, 8, forward_y, 0)

    for index, (source, target, where) in enumerate(halos):
        pltpu.make_async_remote_copy(
            src_ref=source, dst_ref=target, send_sem=send_sem.at[9 + index],
            recv_sem=recv_sem.at[9 + index], device_id=where, device_id_type=MESH,
        ).wait()

    def side(buffer, lane):
        return jnp.concatenate(
            [
                buffer[:, g * group + lane : g * group + lane + 1] + jnp.zeros((64, lanes))
                for g in range(num_groups)
            ],
            axis=0,
        )

    pull(
        spread, sky[...], side(halo_left, group - 1), side(halo_right, 0), halo_below[0:1],
        halo_above[...], halo_bl[0:1, 127:128], halo_ar[7:8, 0:1],
    )

    for index in range(2, 7):
        loads[index].wait()
    total_of(two_r, 4).wait_recv()

    def gather_two(g, carry):
        at = pl.ds(pl.multiple_of(g * 128, 128), 128)
        for c in range(2):
            blocks = [two_r[4 * g + j, c * 32 : (c + 1) * 32] for j in range(4)]
            for k in range(4):
                high, low = split(jnp.concatenate([cut(block, k) for block in blocks], axis=1))
                row = c * 128 + k * 32
                wide[row : row + 32, at] = high
                wide[256 + row : 288 + row, at] = low
        return carry

    lax.fori_loop(0, 8, gather_two, 0)

    def along_x(buffer, half, at):
        cos_part = mul(buffer[...], cxh[:, at])
        sin_part = mul(buffer[...], sxh[:, at])
        cos_part = cos_part[0:half] + cos_part[half:] + mul(buffer[0:half], cxl[:, at])
        sin_part = sin_part[0:half] + sin_part[half:] + mul(buffer[0:half], sxl[:, at])
        q = half // 2
        return cos_part[0:q] + sin_part[q:half], cos_part[q:half] - sin_part[0:q]

    def back_x(buffer, half, rows):
        cos_part = mul_t(buffer[...], cxh[rows])
        sin_part = mul_t(buffer[...], sxh[rows])
        cos_part = cos_part[0:half] + cos_part[half:] + mul_t(buffer[0:half], cxl[rows])
        sin_part = sin_part[0:half] + sin_part[half:] + mul_t(buffer[0:half], sxl[rows])
        q = half // 2
        return cos_part[0:q] - sin_part[q:half], cos_part[q:half] + sin_part[0:q]

    def model(step, carry):
        at = pl.ds(pl.multiple_of(step * 256, 256), 256)
        real, imag = along_x(wide, 256, at)
        sum_real, sum_imag = (0.0, 0.0)
        for k in range(4):
            rows = slice(k * 32, (k + 1) * 32)
            trans_real, trans_imag = (trans[k, 0, :, at], trans[k, 1, :, at])
            sum_real = sum_real + real[rows] * trans_real - imag[rows] * trans_imag
            sum_imag = sum_imag + real[rows] * trans_imag + imag[rows] * trans_real
        for c, part in enumerate((sum_real, sum_imag)):
            high, low = split(part)
            narrow[c * 32 : (c + 1) * 32, at] = high
            narrow[64 + c * 32 : 96 + c * 32, at] = low
        return carry

    lax.fori_loop(0, 4, model, 0)

    def back_three(step, carry):
        part = lax.rem(me // 8 + 1 + step, 4)
        rows = pl.ds(pl.multiple_of(part * 256, 256), 256)
        real, imag = back_x(narrow, 64, rows)
        for j in range(8):
            other = part * 8 + j
            three_s[other] = jnp.concatenate(
                [cut(real[0:16], j), cut(imag[0:16], j), cut(real[16:32], j), cut(imag[16:32], j)],
                axis=1,
            )
            to_all(three_s, three_r, 5, other)
        return carry

    lax.fori_loop(0, 4, back_three, 0)
    loads[7].wait()
    loads[8].wait()
    total_of(seen_r, 2).wait_recv()
    total_of(noise_r, 3).wait_recv()
    total_of(three_r, 5).wait_recv()

    def spread_three(source, carry):
        block = three_r[source]
        where = lane_groups(16)
        for c in range(2):
            for h in range(2):
                high, low = split(jnp.where(where == h * 2 + c, block, 0.0))
                rows = pl.ds(pl.multiple_of(source * 64 + c * 32 + h * 16, 16), 16)
                tall[rows, 0:128] = high
                tall[rows, 128:256] = low
        return carry

    lax.fori_loop(0, devices, spread_three, 0)
    normalizer = 1.0 / (size * size)

    def back_y(rows):
        both = mul(gh[rows], tall[...])
        out = both[:, 0:128] + both[:, 128:256] + mul(gl[rows], tall[:, 0:128])
        return out * normalizer

    def residual(step, carry):
        band = lax.rem(my_y + 1 + step, bands)
        rows = pl.ds(pl.multiple_of(band * 256, 256), 256)
        out = fold(back_y(rows))
        blurred = pick_groups([out[g * 64 : (g + 1) * 64] for g in range(num_groups)])
        left_over = noise_r[band] * (blurred - seen_r[band])
        res_s[band] = left_over
        for g in range(num_groups):
            high, low = split(jnp.concatenate([cut(left_over, g)] * num_groups, axis=1))
            rows = pl.ds(pl.multiple_of(band * 256 + g * 64, 64), 64)
            fields[rows, 0:128] = high
            fields[rows, 128:256] = low
        return carry

    lax.fori_loop(0, bands, residual, 0)

    def forward_four(step, carry):
        part, out = along_y(step)
        for j in range(4):
            other = part * 4 + j
            pieces = []
            for h in range(2):
                for c in range(2):
                    row = j * 64 + c * 32 + h * 16
                    pieces.append(out[row : row + 16])
            four_s[other] = pick_groups(pieces)
            to_all(four_s, four_r, 6, other)
        return carry

    lax.fori_loop(0, 8, forward_four, 0)
    for other in range(bands):
        to_band(res_s, res_r, 8, other)
    total_of(four_r, 6).wait_recv()

    def gather_four(g, carry):
        at = pl.ds(pl.multiple_of(g * 128, 128), 128)
        blocks = [four_r[4 * g + j] for j in range(4)]
        for c in range(2):
            for h in range(2):
                high, low = split(
                    jnp.concatenate([cut(block, h * 2 + c) for block in blocks], axis=1)
                )
                row = c * 32 + h * 16
                narrow[row : row + 16, at] = high
                narrow[64 + row : 80 + row, at] = low
        return carry

    lax.fori_loop(0, 8, gather_four, 0)

    def adjoint(step, carry):
        at = pl.ds(pl.multiple_of(step * 256, 256), 256)
        real, imag = along_x(narrow, 64, at)
        for k in range(4):
            trans_real, trans_imag = (trans[k, 0, :, at], trans[k, 1, :, at])
            both = (real * trans_real + imag * trans_imag, imag * trans_real - real * trans_imag)
            for c in range(2):
                high, low = split(both[c])
                row = c * 128 + k * 32
                wide[row : row + 32, at] = high
                wide[256 + row : 288 + row, at] = low
        return carry

    lax.fori_loop(0, 4, adjoint, 0)

    def back_five(step, carry):
        part = lax.rem(me // 8 + 1 + step, 4)
        rows = pl.ds(pl.multiple_of(part * 256, 256), 256)
        both = back_x(wide, 256, rows)
        for j in range(8):
            other = part * 8 + j
            for c in range(2):
                five_s[other, c * 32 : (c + 1) * 32] = jnp.concatenate(
                    [cut(both[c][k * 32 : (k + 1) * 32], j) for k in range(4)], axis=1
                )
            to_all(five_s, five_r, 7, other)
        return carry

    lax.fori_loop(0, 4, back_five, 0)
    total_of(five_r, 7).wait_recv()

    def split_five(source, carry):
        high, low = split(five_r[source])
        rows = pl.ds(pl.multiple_of(source * 64, 64), 64)
        tall[rows, 0:128] = high
        tall[rows, 128:256] = low
        return carry

    lax.fori_loop(0, devices, split_five, 0)

    def finish(step, carry):
        band = lax.rem(my_y + 1 + step, bands)
        rows = pl.ds(pl.multiple_of(band * 256, 256), 256)
        out = fold(back_y(rows) * weights[rows])
        grad_s[band] = pick_groups([out[g * 64 : (g + 1) * 64] for g in range(num_groups)])
        to_band(grad_s, grad_r, 15, band)
        return carry

    lax.fori_loop(0, bands, finish, 0)
    total_of(res_r, 8).wait_recv()
    total_of(grad_r, 15).wait_recv()
    for g in range(num_groups):
        rows = slice(g * 64, (g + 1) * 64)
        res_out[rows] = jnp.concatenate([cut(res_r[band], g) for band in range(bands)], axis=1)
        grad_out[rows] = (
            jnp.concatenate([cut(grad_r[band], g) for band in range(bands)], axis=1)
            - tv_weight * spread[rows]
        )
    for buffer, phase in (
        (sky_s, 0), (tile_s, 1), (seen_s, 2), (noise_s, 3), (two_s, 4), (three_s, 5),
        (four_s, 6), (five_s, 7), (res_s, 8), (grad_s, 15),
    ):
        total_of(buffer, phase).wait_send()


def on_device(sky_image, observed, noise_weight, basis_tiles, intersection, counts, transfer):
    pool, tile_side = (basis_tiles.shape[0], basis_tiles.shape[1])
    shape = (lax.axis_size("sy"), lax.axis_size("sx"), *sky_image.shape, pool, tile_side)
    if shape + intersection.shape[2:] != (bands, band_size, 256, lanes, 4, lanes, 4):
        return generic_device(
            sky_image, observed, noise_weight, basis_tiles, intersection, counts, transfer
        )
    my_band, my_column = (lax.axis_index("sy"), lax.axis_index("sx"))
    lists = intersection.reshape(bands, 2, band_size, 4).transpose(0, 2, 1, 3)
    lists = lists.reshape(bands, band_size, 8)
    slots = jnp.arange(2, dtype=jnp.int32)
    asked = lax.dynamic_index_in_dim(lists, my_band, 0, False)
    local = asked - (my_band * band_size + my_column) * pool
    hit = (local >= 0) & (local < pool)
    earlier = np.tril(np.ones((8, 8), bool), -1)
    rank = jnp.sum((hit[:, None, :] & earlier).astype(jnp.int32), axis=2)
    chosen = (
        hit[:, :, None, None]
        & (local[:, :, None, None] == jnp.arange(pool, dtype=jnp.int32)[:, None])
        & (rank[:, :, None, None] == slots)
    ).any(axis=1)
    tile_mult = jnp.broadcast_to(
        chosen.astype(jnp.float32)[:, :, None, :, None], (band_size, pool, 2, 2, group)
    ).reshape(band_size, pool, lanes)
    wanted = lax.dynamic_index_in_dim(lists, my_column, 1, False)
    holder = wanted // pool - jnp.arange(bands, dtype=jnp.int32)[:, None] * band_size
    same = holder[:, :, None] == holder[:, None, :]
    place = jnp.sum((same & earlier).astype(jnp.int32), axis=2)
    pick = (holder[:, :, None, None] == jnp.arange(band_size, dtype=jnp.int32)[:, None]) & (
        place[:, :, None, None] == slots
    )
    pick_mult = jnp.broadcast_to(
        pick.astype(jnp.float32)[:, :, :, None, :, None], (bands, 8, band_size, 2, 2, group)
    ).reshape(bands * 8, band_size, lanes)
    in_use = (jnp.arange(4, dtype=jnp.int32) < counts.reshape(2, 1)).reshape(8, 1)
    mask = jnp.broadcast_to(in_use.astype(jnp.float32), (8, lanes))
    constants = tables()
    f32, bf16 = (jnp.float32, jnp.bfloat16)

    def double(*dims, kind=f32):
        return [pltpu.VMEM(dims, kind)] * 2

    scratch = [
        pltpu.VMEM(transfer.shape, f32),
        *[pltpu.VMEM(table.shape, bf16) for table in constants],
        *double(bands, 72, lanes),
        *double(bands, 64, lanes),
        *double(bands, 64, lanes),
        *double(devices, 64, lanes, kind=bf16),
        *double(devices, 64, lanes),
        *double(devices, 16, lanes),
        *double(devices, 16, lanes),
        *double(devices, 64, lanes),
        *double(bands, 64, lanes),
        *double(bands, 64, lanes),
        *double(64, lanes),
        *double(8, lanes),
        *double(8, lanes),
        pltpu.VMEM((size, lanes), f32),
        pltpu.VMEM((size, 2 * lanes), bf16),
        pltpu.VMEM((512, size), bf16),
        pltpu.VMEM((128, size), bf16),
        pltpu.VMEM((2 * size, 2 * lanes), bf16),
        pltpu.VMEM((256, lanes), f32),
        pltpu.SemaphoreType.DMA((9,)),
        pltpu.SemaphoreType.DMA((16,)),
        pltpu.SemaphoreType.DMA((16,)),
    ]
    in_vmem = pl.BlockSpec(memory_space=pltpu.VMEM)
    outside = pl.BlockSpec(memory_space=pl.ANY)
    return pl.pallas_call(
        kernel,
        out_shape=[jax.ShapeDtypeStruct(sky_image.shape, f32)] * 2,
        in_specs=[in_vmem] * 7 + [outside] * 9,
        out_specs=[in_vmem] * 2,
        scratch_shapes=scratch,
        compiler_params=pltpu.CompilerParams(
            collective_id=0, has_side_effects=True, vmem_limit_bytes=56 * 1024 * 1024
        ),
        cost_estimate=pl.CostEstimate(
            flops=10_000_000_000, bytes_accessed=30_000_000, transcendentals=0
        ),
    )(
        sky_image, observed, noise_weight, mask, basis_tiles, tile_mult, pick_mult,
        transfer, *(jnp.asarray(table) for table in constants),
    )


def solution(mesh):
    placed = (
        P("sy", "sx"),
        P("sy", "sx"),
        P("sy", "sx"),
        P(("sy", "sx"), None, None),
        P(),
        P("sy", "sx"),
        P(None, None, ("sy", "sx"), None),
    )
    return jax.shard_map(
        on_device,
        mesh=mesh,
        in_specs=placed,
        out_specs=(P("sy", "sx"), P("sy", "sx")),
        check_vma=False,
    )
```

```python
import jax
import jax.numpy as jnp
import numpy as np
from jax import lax
from jax.experimental import pallas as pl
from jax.experimental.pallas import tpu as pltpu
from jax.sharding import PartitionSpec as P

radix = 128
highest = lax.Precision.HIGHEST
tv_weight = 0.5
smoothing = 0.25


def with_halo(block, sides, width):
    for axis, dim in sides:
        count = lax.axis_size(axis)
        forward = [(i, i + 1) for i in range(count - 1)]
        forward.append((count - 1, 0))
        backward = [(target, source) for source, target in forward]
        low = lax.ppermute(
            lax.slice_in_dim(block, block.shape[dim] - width, None, axis=dim), axis, forward
        )
        high = lax.ppermute(lax.slice_in_dim(block, 0, width, axis=dim), axis, backward)
        block = jnp.concatenate([low, block, high], axis=dim)
    return block


def circle(left_index, right_index, length, orient):
    product = left_index[:, None] * right_index[None, :] % length
    angles = product.astype(jnp.float32) * (2.0 * jnp.pi / length)
    return (jnp.cos(angles), orient * jnp.sin(angles))


def contract(pattern, operand, matrix):
    return jnp.einsum(pattern, operand, matrix, precision=highest)


def forward_last(stacked):
    num_parts, num_fields, num_lines, length = stacked.shape
    short_size = length // radix
    pieces = stacked.reshape(num_parts, num_fields, num_lines, short_size, radix)
    short_index = jnp.arange(short_size, dtype=jnp.int32)
    long_index = jnp.arange(radix, dtype=jnp.int32)
    cos_short, sin_short = circle(short_index, short_index, short_size, -1.0)
    cos_turn, sin_turn = circle(short_index, long_index, length, -1.0)
    cos_long, sin_long = circle(long_index, long_index, radix, -1.0)
    first_form = "fmba,bk->fmka"
    real_part = contract(first_form, pieces[0], cos_short)
    imag_part = contract(first_form, pieces[0], sin_short)
    if num_parts == 2:
        real_part = real_part - contract(first_form, pieces[1], sin_short)
        imag_part = imag_part + contract(first_form, pieces[1], cos_short)
    turned_real = real_part * cos_turn - imag_part * sin_turn
    turned_imag = real_part * sin_turn + imag_part * cos_turn
    second_form = "fmka,aj->fmkj"
    out_real = contract(second_form, turned_real, cos_long) - contract(
        second_form, turned_imag, sin_long
    )
    out_imag = contract(second_form, turned_real, sin_long) + contract(
        second_form, turned_imag, cos_long
    )
    return jnp.stack([out_real, out_imag]).reshape(2, num_fields, num_lines, length)


def inverse_last(stacked, real_only):
    num_fields, num_lines, length = (stacked.shape[1], stacked.shape[2], stacked.shape[3])
    short_size = length // radix
    pieces = stacked.reshape(2, num_fields, num_lines, short_size, radix)
    short_index = jnp.arange(short_size, dtype=jnp.int32)
    long_index = jnp.arange(radix, dtype=jnp.int32)
    cos_long, sin_long = circle(long_index, long_index, radix, 1.0)
    cos_turn, sin_turn = circle(short_index, long_index, length, 1.0)
    cos_short, sin_short = circle(short_index, short_index, short_size, 1.0)
    first_form = "fmkj,ja->fmka"
    real_part = contract(first_form, pieces[0], cos_long) - contract(
        first_form, pieces[1], sin_long
    )
    imag_part = contract(first_form, pieces[0], sin_long) + contract(
        first_form, pieces[1], cos_long
    )
    turned_real = real_part * cos_turn - imag_part * sin_turn
    turned_imag = real_part * sin_turn + imag_part * cos_turn
    second_form = "fmka,kb->fmba"
    out_real = contract(second_form, turned_real, cos_short) - contract(
        second_form, turned_imag, sin_short
    )
    if real_only:
        return out_real.reshape(1, num_fields, num_lines, length)
    out_imag = contract(second_form, turned_real, sin_short) + contract(
        second_form, turned_imag, cos_short
    )
    return jnp.stack([out_real, out_imag]).reshape(2, num_fields, num_lines, length)


def to_spectra(pixels):
    columns = lax.all_to_all(
        jnp.swapaxes(pixels, 2, 3), "sy", split_axis=2, concat_axis=3, tiled=True
    )
    along_y = forward_last(columns)
    blocks = lax.all_to_all(along_y, "sy", split_axis=3, concat_axis=2, tiled=True)
    lines = lax.all_to_all(
        jnp.swapaxes(blocks, 2, 3), "sx", split_axis=2, concat_axis=3, tiled=True
    )
    return forward_last(lines)


def from_spectra(spectrum, normalizer):
    along_x = inverse_last(spectrum, False)
    blocks = lax.all_to_all(along_x, "sx", split_axis=3, concat_axis=2, tiled=True)
    columns = lax.all_to_all(
        jnp.swapaxes(blocks, 2, 3), "sy", split_axis=2, concat_axis=3, tiled=True
    )
    values = inverse_last(columns, True) * normalizer
    pixel_blocks = lax.all_to_all(values, "sy", split_axis=3, concat_axis=2, tiled=True)
    return jnp.swapaxes(pixel_blocks, 2, 3)[0]


def generic_device(sky_image, observed, noise_weight, basis_tiles, intersection, counts, transfer):
    height, breadth = sky_image.shape
    pool_size, tile_side = (basis_tiles.shape[0], basis_tiles.shape[1])
    components = intersection.shape[2]
    tiles_down = height // tile_side
    tiles_across = breadth // tile_side
    band_size = lax.axis_size("sx")
    sky_row = lax.axis_index("sy")
    sky_column = lax.axis_index("sx")
    num_requests = tiles_down * tiles_across * components
    zero_index = jnp.zeros((), jnp.int32)
    own_lists = lax.dynamic_slice(
        intersection,
        (sky_row * tiles_down, sky_column * tiles_across, zero_index),
        (tiles_down, tiles_across, components),
    ).reshape(num_requests)
    band_start = sky_row * band_size * pool_size
    band_index = own_lists - band_start
    flat_tiles = basis_tiles.reshape(pool_size, tile_side * tile_side)
    piece = lax.all_gather(flat_tiles, "sx", axis=0, tiled=True)
    piece_count = piece.shape[0]
    hits = (band_index[:, None] == jnp.arange(piece_count, dtype=jnp.int32)[None, :]).astype(
        jnp.bfloat16
    )
    coefficient = jnp.dot(hits, piece, preferred_element_type=jnp.float32)
    in_use = (jnp.arange(components, dtype=jnp.int32)[None, None, :] < counts[:, :, None]).astype(
        jnp.float32
    )
    coef_maps = (
        coefficient.reshape(tiles_down, tiles_across, components, tile_side, tile_side)
        * in_use[:, :, :, None, None]
    )
    weights = coef_maps.transpose(2, 0, 3, 1, 4).reshape(components, height, breadth)
    normalizer = 1.0 / (transfer.shape[2] * lax.axis_size("sy") * band_size * transfer.shape[3])
    spectra = to_spectra((weights * sky_image[None])[None])
    trans_real = transfer[:, 0]
    trans_imag = transfer[:, 1]
    model_real = jnp.sum(spectra[0] * trans_real - spectra[1] * trans_imag, axis=0)
    model_imag = jnp.sum(spectra[0] * trans_imag + spectra[1] * trans_real, axis=0)
    blurred = from_spectra(jnp.stack([model_real, model_imag])[:, None], normalizer)[0]
    residual = noise_weight * (blurred - observed)
    back_spectrum = to_spectra(residual[None, None])
    pull_real = back_spectrum[0] * trans_real + back_spectrum[1] * trans_imag
    pull_imag = back_spectrum[1] * trans_real - back_spectrum[0] * trans_imag
    pulled = from_spectra(jnp.stack([pull_real, pull_imag]), normalizer)
    data_grad = jnp.sum(weights * pulled, axis=0)
    framed = with_halo(sky_image, (("sy", 0), ("sx", 1)), 1)
    step_x = framed[:-1, 1:] - framed[:-1, :-1]
    step_y = framed[1:, :-1] - framed[:-1, :-1]
    magnitude = jnp.sqrt(step_x * step_x + step_y * step_y + smoothing)
    flow_x = step_x / magnitude
    flow_y = step_y / magnitude
    spread = flow_x[1:, 1:] - flow_x[1:, :-1] + flow_y[1:, 1:] - flow_y[:-1, 1:]
    gradient = data_grad - tv_weight * spread
    return (residual, gradient)


lanes = 128
group = 32
num_groups = 4
bands = 4
band_size = 8
devices = 32
size = 1024
MESH = pl.DeviceIdType.MESH


def split_table(values):
    high = values.astype(jnp.bfloat16)
    return high, (values - high.astype(np.float64)).astype(jnp.bfloat16)


def tables():
    spot = np.arange(size)
    owner, column = (spot // group, spot % group)
    pixel = (owner % band_size) * lanes + (owner // band_size) * group + column
    frequency = (size // radix) * (spot % radix) + spot // radix
    angle = (frequency[:, None] * spot[None, :] % size) * (2.0 * np.pi / size)
    parts = np.stack([np.cos(angle), -np.sin(angle)]).reshape(2, devices, group, size)
    along_y = parts.transpose(1, 0, 2, 3).reshape(2 * size, size)
    angle = (pixel[:, None] * frequency[None, :] % size) * (2.0 * np.pi / size)
    cos_high, cos_low = split_table(np.cos(angle))
    sin_high, sin_low = split_table(np.sin(angle))
    return (
        *split_table(along_y),
        cos_high,
        sin_high,
        cos_low,
        sin_low,
        *split_table(np.ascontiguousarray(along_y.T)),
    )


def split(values):
    high = values.astype(jnp.bfloat16)
    return high, (values - high.astype(jnp.float32)).astype(jnp.bfloat16)


def mul(left, right):
    return jnp.dot(left, right, preferred_element_type=jnp.float32)


def mul_t(left, right):
    return lax.dot_general(
        left, right, (((1,), (1,)), ((), ())), preferred_element_type=jnp.float32
    )


def cut(values, index):
    return values[:, index * group : (index + 1) * group]


def lane_groups(rows):
    return lax.broadcasted_iota(jnp.int32, (rows, lanes), 1) // group


def pick_groups(pieces):
    where = lane_groups(pieces[0].shape[0])
    out = pieces[0]
    for index in range(1, num_groups):
        out = jnp.where(where == index, pieces[index], out)
    return out


def fold(values):
    values = values + pltpu.roll(values, 64, 1)
    return values + pltpu.roll(values, 32, 1)


def encode(real, imag):
    largest = jnp.max(jnp.maximum(jnp.abs(real), jnp.abs(imag)), axis=0, keepdims=True)
    level = jnp.ceil(jnp.log2(jnp.maximum(largest, 1e-30)) * 256.0 + 0.01)
    factor = 32760.0 * jnp.exp2(level * (-1.0 / 256.0))
    high = jnp.floor(real * factor + 0.5).astype(jnp.int32)
    low = jnp.floor(imag * factor + 0.5).astype(jnp.int32)
    return high * 65536 + (low + 32768), level.astype(jnp.int32)


def decode(packed, level):
    factor = jnp.exp2(level.astype(jnp.float32) * (1.0 / 256.0)) * (1.0 / 32760.0)
    real = (packed >> 16).astype(jnp.float32) * factor
    imag = ((packed & 65535) - 32768).astype(jnp.float32) * factor
    return real, imag


def pull(total, sky, left, right, below, above, below_left, above_right):
    rows = sky.shape[0]
    lane = lax.broadcasted_iota(jnp.int32, sky.shape, 1)
    row = lax.broadcasted_iota(jnp.int32, sky.shape, 0)

    def flows(step_x, step_y):
        magnitude = jnp.sqrt(step_x * step_x + step_y * step_y + smoothing)
        return step_x / magnitude, step_y / magnitude

    next_x = jnp.where(lane == lanes - 1, right, pltpu.roll(sky, lanes - 1, 1))
    next_y = jnp.where(row == rows - 1, below, pltpu.roll(sky, rows - 1, 0))
    flow_x, flow_y = flows(next_x - sky, next_y - sky)
    left_next = jnp.where(row == rows - 1, below_left, pltpu.roll(left, rows - 1, 0))
    side_x, _ = flows(sky - left, left_next - left)
    side_x = side_x[:, 0:1]
    above_next = jnp.where(lane[0:8] == lanes - 1, above_right, pltpu.roll(above, lanes - 1, 1))
    _, top_y = flows(above_next - above, sky[0:1] - above)
    before_x = jnp.where(lane == 0, side_x, pltpu.roll(flow_x, 1, 1))
    before_y = jnp.where(row == 0, top_y[7:8], pltpu.roll(flow_y, 1, 0))
    total[...] = flow_x - before_x + flow_y - before_y


def kernel(
    sky, seen, noise, basis, lists, counts,
    trans_hbm, fyh_hbm, fyl_hbm, cxh_hbm, sxh_hbm, cxl_hbm, sxl_hbm, gh_hbm, gl_hbm,
    res_out, grad_out,
    trans, fyh, fyl, cxh, sxh, cxl, sxl, gh, gl,
    sky_s, sky_r, seen_s, seen_r, noise_s, noise_r, tile_s, tile_r,
    two_s, two_r, three_s, three_r, four_s, four_r, five_s, five_r,
    res_s, res_r, grad_s, grad_r,
    halo_left, halo_right, halo_below, halo_above, halo_bl, halo_ar,
    weights, fields, wide, narrow, tall, spread,
    load_sem, send_sem, recv_sem,
):
    my_y, my_x = (lax.axis_index("sy"), lax.axis_index("sx"))
    me = my_y * band_size + my_x
    barrier = pltpu.get_barrier_semaphore()

    def greet(step, carry):
        other = lax.rem(me + step, devices)
        pl.semaphore_signal(
            barrier, inc=1, device_id=(other // band_size, lax.rem(other, band_size)),
            device_id_type=MESH,
        )
        return carry

    lax.fori_loop(1, devices, greet, 0)
    loads = []
    pairs = (
        (fyh_hbm, fyh), (fyl_hbm, fyl), (cxh_hbm, cxh), (sxh_hbm, sxh), (cxl_hbm, cxl),
        (sxl_hbm, sxl), (trans_hbm, trans), (gh_hbm, gh), (gl_hbm, gl),
    )
    for index, (source, target) in enumerate(pairs):
        loads.append(pltpu.make_async_copy(source, target, load_sem.at[index]))
        loads[-1].start()

    def send(source, target, phase, where):
        pltpu.make_async_remote_copy(
            src_ref=source, dst_ref=target, send_sem=send_sem.at[phase],
            recv_sem=recv_sem.at[phase], device_id=where, device_id_type=MESH,
        ).start()

    def total_of(buffer, phase):
        part = buffer.at[pl.ds(0, buffer.shape[0] - 1)]
        return pltpu.make_async_remote_copy(
            src_ref=part, dst_ref=part, send_sem=send_sem.at[phase],
            recv_sem=recv_sem.at[phase], device_id=(lax.rem(my_y + 1, bands), my_x),
            device_id_type=MESH,
        )

    def to_all(source, target, phase, other):
        @pl.when(other != me)
        def _():
            send(
                source.at[other], target.at[me], phase,
                (other // band_size, lax.rem(other, band_size)),
            )

        @pl.when(other == me)
        def _():
            target[me] = source[me]

    def to_band(source, target, phase, other):
        @pl.when(other != my_y)
        def _():
            send(source.at[other], target.at[my_y], phase, (other, my_x))

        @pl.when(other == my_y)
        def _():
            target[my_y] = source[my_y]

    def pack(block, other):
        return jnp.concatenate(
            [cut(block[g * 64 : (g + 1) * 64], other) for g in range(num_groups)], axis=1
        )

    row = lax.broadcasted_iota(jnp.int32, (8, lanes), 0)
    mask = jnp.where(row % 4 < jnp.where(row < 4, counts[0, 0], counts[1, 0]), 1.0, 0.0)
    slot_lane = lane_groups(64) % 2
    for other in range(bands):
        sky_s[other, 0:64] = pack(sky[...], other)
        sky_s[other, 64:72] = mask
    pl.semaphore_wait(barrier, devices - 1)
    for other in range(bands):
        to_band(sky_s, sky_r, 0, other)

    for other in range(bands):
        packs = []
        for t in range(4):
            part = cut(basis[t].astype(jnp.float32), other)
            packs.append(
                jnp.concatenate([part[0:64], part[0:64], part[64:128], part[64:128]], axis=1)
            )

        def choose(column, carry):
            first, second, seen_before = (-1, -1, 0)
            for e in range(8):
                local = lists[my_y * 2 + e // 4, column, e % 4] - me * 4
                hit = (local >= 0) & (local < 4)
                first = jnp.where(hit & (seen_before == 0), local, first)
                second = jnp.where(hit & (seen_before == 1), local, second)
                seen_before = seen_before + jnp.where(hit, 1, 0)
            wanted = jnp.where(slot_lane == 0, first, second)
            acc = jnp.where(wanted == 0, packs[0], 0.0)
            for t in range(1, 4):
                acc = jnp.where(wanted == t, packs[t], acc)
            tile_s[other * band_size + column] = acc.astype(jnp.bfloat16)
            to_all(tile_s, tile_r, 1, other * band_size + column)
            return carry

        lax.fori_loop(0, band_size, choose, 0)

    for other in range(bands):
        seen_s[other] = pack(seen[...], other)
        noise_s[other] = pack(noise[...], other)
        to_band(seen_s, seen_r, 2, other)
        to_band(noise_s, noise_r, 3, other)
    up, down = (lax.rem(my_y + bands - 1, bands), lax.rem(my_y + 1, bands))
    west, east = (lax.rem(my_x + band_size - 1, band_size), lax.rem(my_x + 1, band_size))
    first, last = (sky.at[pl.ds(0, 8)], sky.at[pl.ds(248, 8)])
    halos = (
        (sky_s.at[0, pl.ds(0, 64)], halo_right, (my_y, west)),
        (sky_s.at[bands - 1, pl.ds(0, 64)], halo_left, (my_y, east)),
        (first, halo_below, (up, my_x)),
        (first, halo_bl, (up, east)),
        (last, halo_above, (down, my_x)),
        (last, halo_ar, (down, west)),
    )
    for index, (source, target, where) in enumerate(halos):
        send(source, target, 9 + index, where)

    total_of(sky_r, 0).wait_recv()
    total_of(tile_r, 1).wait_recv()

    def weigh(band, carry):
        parts = []
        tiles = [tile_r[band * band_size + h].astype(jnp.float32) for h in range(band_size)]
        holders = [
            lists[band * 2 + e // 4, my_x, e % 4] // 4 - band * band_size for e in range(8)
        ]
        for e in range(8):
            slot = 0
            for earlier in range(e):
                slot = slot + jnp.where(holders[earlier] == holders[e], 1, 0)
            place = holders[e] * 2 + slot
            acc = jnp.zeros((64, lanes), jnp.float32)
            for h in range(band_size):
                acc = jnp.where(slot_lane + 2 * h == place, tiles[h], acc)
            acc = (acc + pltpu.roll(acc, 96, 1)) * sky_r[band, 64 + e : 65 + e]
            parts.append(acc)
        for g in range(num_groups):
            down_tile, half = (g // 2, g % 2)
            block = jnp.concatenate(
                [cut(parts[down_tile * 4 + k], 2 * half) for k in range(4)], axis=1
            )
            rows = pl.ds(pl.multiple_of(band * 256 + g * 64, 64), 64)
            weights[rows] = block
            high, low = split(
                block * jnp.concatenate([cut(sky_r[band, 0:64], g)] * num_groups, axis=1)
            )
            fields[rows, 0:128] = high
            fields[rows, 128:256] = low
        return carry

    lax.fori_loop(0, bands, weigh, 0)
    loads[0].wait()
    loads[1].wait()

    def along_y(step):
        part = lax.rem(me // 4 + 1 + step, 8)
        rows = pl.ds(pl.multiple_of(part * 256, 256), 256)
        both = mul(fyh[rows], fields[...])
        return part, both[:, 0:128] + both[:, 128:256] + mul(fyl[rows], fields[:, 0:128])

    def forward_y(step, carry):
        part, out = along_y(step)
        for j in range(4):
            other = part * 4 + j
            packed, level = encode(out[j * 64 : j * 64 + 32], out[j * 64 + 32 : j * 64 + 64])
            two_s[other, 0:32] = packed
            two_s[other, 32:40] = jnp.broadcast_to(level, (8, lanes))
            to_all(two_s, two_r, 4, other)
        return carry

    lax.fori_loop(0, 8, forward_y, 0)

    for index, (source, target, where) in enumerate(halos):
        pltpu.make_async_remote_copy(
            src_ref=source, dst_ref=target, send_sem=send_sem.at[9 + index],
            recv_sem=recv_sem.at[9 + index], device_id=where, device_id_type=MESH,
        ).wait()

    def side(buffer, lane):
        return jnp.concatenate(
            [
                buffer[:, g * group + lane : g * group + lane + 1] + jnp.zeros((64, lanes))
                for g in range(num_groups)
            ],
            axis=0,
        )

    pull(
        spread, sky[...], side(halo_left, group - 1), side(halo_right, 0), halo_below[0:1],
        halo_above[...], halo_bl[0:1, 127:128], halo_ar[7:8, 0:1],
    )

    for index in range(2, 7):
        loads[index].wait()
    total_of(two_r, 4).wait_recv()

    def gather_two(g, carry):
        at = pl.ds(pl.multiple_of(g * 128, 128), 128)
        parts = [decode(two_r[4 * g + j, 0:32], two_r[4 * g + j, 32:33]) for j in range(4)]
        for c in range(2):
            blocks = [part[c] for part in parts]
            for k in range(4):
                high, low = split(jnp.concatenate([cut(block, k) for block in blocks], axis=1))
                row = c * 128 + k * 32
                wide[row : row + 32, at] = high
                wide[256 + row : 288 + row, at] = low
        return carry

    lax.fori_loop(0, 8, gather_two, 0)

    def along_x(buffer, half, at):
        cos_part = mul(buffer[...], cxh[:, at])
        sin_part = mul(buffer[...], sxh[:, at])
        cos_part = cos_part[0:half] + cos_part[half:] + mul(buffer[0:half], cxl[:, at])
        sin_part = sin_part[0:half] + sin_part[half:] + mul(buffer[0:half], sxl[:, at])
        q = half // 2
        return cos_part[0:q] + sin_part[q:half], cos_part[q:half] - sin_part[0:q]

    def back_x(buffer, half, rows):
        cos_part = mul_t(buffer[...], cxh[rows])
        sin_part = mul_t(buffer[...], sxh[rows])
        cos_part = cos_part[0:half] + cos_part[half:] + mul_t(buffer[0:half], cxl[rows])
        sin_part = sin_part[0:half] + sin_part[half:] + mul_t(buffer[0:half], sxl[rows])
        q = half // 2
        return cos_part[0:q] - sin_part[q:half], cos_part[q:half] + sin_part[0:q]

    def model(step, carry):
        at = pl.ds(pl.multiple_of(step * 256, 256), 256)
        real, imag = along_x(wide, 256, at)
        sum_real, sum_imag = (0.0, 0.0)
        for k in range(4):
            rows = slice(k * 32, (k + 1) * 32)
            trans_real, trans_imag = (trans[k, 0, :, at], trans[k, 1, :, at])
            sum_real = sum_real + real[rows] * trans_real - imag[rows] * trans_imag
            sum_imag = sum_imag + real[rows] * trans_imag + imag[rows] * trans_real
        for c, part in enumerate((sum_real, sum_imag)):
            high, low = split(part)
            narrow[c * 32 : (c + 1) * 32, at] = high
            narrow[64 + c * 32 : 96 + c * 32, at] = low
        return carry

    lax.fori_loop(0, 4, model, 0)

    def back_three(step, carry):
        part = lax.rem(me // 8 + 1 + step, 4)
        rows = pl.ds(pl.multiple_of(part * 256, 256), 256)
        real, imag = back_x(narrow, 64, rows)
        for j in range(8):
            other = part * 8 + j
            three_s[other] = jnp.concatenate(
                [cut(real[0:16], j), cut(imag[0:16], j), cut(real[16:32], j), cut(imag[16:32], j)],
                axis=1,
            )
            to_all(three_s, three_r, 5, other)
        return carry

    lax.fori_loop(0, 4, back_three, 0)
    loads[7].wait()
    loads[8].wait()
    total_of(seen_r, 2).wait_recv()
    total_of(noise_r, 3).wait_recv()
    total_of(three_r, 5).wait_recv()

    def spread_three(source, carry):
        block = three_r[source]
        where = lane_groups(16)
        for c in range(2):
            for h in range(2):
                high, low = split(jnp.where(where == h * 2 + c, block, 0.0))
                rows = pl.ds(pl.multiple_of(source * 64 + c * 32 + h * 16, 16), 16)
                tall[rows, 0:128] = high
                tall[rows, 128:256] = low
        return carry

    lax.fori_loop(0, devices, spread_three, 0)
    normalizer = 1.0 / (size * size)

    def back_y(rows):
        both = mul(gh[rows], tall[...])
        out = both[:, 0:128] + both[:, 128:256] + mul(gl[rows], tall[:, 0:128])
        return out * normalizer

    def residual(step, carry):
        band = lax.rem(my_y + 1 + step, bands)
        rows = pl.ds(pl.multiple_of(band * 256, 256), 256)
        out = fold(back_y(rows))
        blurred = pick_groups([out[g * 64 : (g + 1) * 64] for g in range(num_groups)])
        left_over = noise_r[band] * (blurred - seen_r[band])
        res_s[band] = left_over
        for g in range(num_groups):
            high, low = split(jnp.concatenate([cut(left_over, g)] * num_groups, axis=1))
            rows = pl.ds(pl.multiple_of(band * 256 + g * 64, 64), 64)
            fields[rows, 0:128] = high
            fields[rows, 128:256] = low
        return carry

    lax.fori_loop(0, bands, residual, 0)

    def forward_four(step, carry):
        part, out = along_y(step)
        for j in range(4):
            other = part * 4 + j
            pieces = []
            for h in range(2):
                for c in range(2):
                    row = j * 64 + c * 32 + h * 16
                    pieces.append(out[row : row + 16])
            four_s[other] = pick_groups(pieces)
            to_all(four_s, four_r, 6, other)
        return carry

    lax.fori_loop(0, 8, forward_four, 0)
    for other in range(bands):
        to_band(res_s, res_r, 8, other)
    total_of(four_r, 6).wait_recv()

    def gather_four(g, carry):
        at = pl.ds(pl.multiple_of(g * 128, 128), 128)
        blocks = [four_r[4 * g + j] for j in range(4)]
        for c in range(2):
            for h in range(2):
                high, low = split(
                    jnp.concatenate([cut(block, h * 2 + c) for block in blocks], axis=1)
                )
                row = c * 32 + h * 16
                narrow[row : row + 16, at] = high
                narrow[64 + row : 80 + row, at] = low
        return carry

    lax.fori_loop(0, 8, gather_four, 0)

    def adjoint(step, carry):
        at = pl.ds(pl.multiple_of(step * 256, 256), 256)
        real, imag = along_x(narrow, 64, at)
        for k in range(4):
            trans_real, trans_imag = (trans[k, 0, :, at], trans[k, 1, :, at])
            both = (real * trans_real + imag * trans_imag, imag * trans_real - real * trans_imag)
            for c in range(2):
                high, low = split(both[c])
                row = c * 128 + k * 32
                wide[row : row + 32, at] = high
                wide[256 + row : 288 + row, at] = low
        return carry

    lax.fori_loop(0, 4, adjoint, 0)

    def back_five(step, carry):
        part = lax.rem(me // 8 + 1 + step, 4)
        rows = pl.ds(pl.multiple_of(part * 256, 256), 256)
        both = back_x(wide, 256, rows)
        for j in range(8):
            other = part * 8 + j
            real, imag = [
                jnp.concatenate([cut(part[k * 32 : (k + 1) * 32], j) for k in range(4)], axis=1)
                for part in both
            ]
            packed, level = encode(real, imag)
            five_s[other, 0:32] = packed
            five_s[other, 32:40] = jnp.broadcast_to(level, (8, lanes))
            to_all(five_s, five_r, 7, other)
        return carry

    lax.fori_loop(0, 4, back_five, 0)
    total_of(five_r, 7).wait_recv()

    def split_five(source, carry):
        parts = decode(five_r[source, 0:32], five_r[source, 32:33])
        for c in range(2):
            high, low = split(parts[c])
            rows = pl.ds(pl.multiple_of(source * 64 + c * 32, 32), 32)
            tall[rows, 0:128] = high
            tall[rows, 128:256] = low
        return carry

    lax.fori_loop(0, devices, split_five, 0)

    def finish(step, carry):
        band = lax.rem(my_y + 1 + step, bands)
        rows = pl.ds(pl.multiple_of(band * 256, 256), 256)
        out = fold(back_y(rows) * weights[rows])
        grad_s[band] = pick_groups([out[g * 64 : (g + 1) * 64] for g in range(num_groups)])
        to_band(grad_s, grad_r, 15, band)
        return carry

    lax.fori_loop(0, bands, finish, 0)
    total_of(res_r, 8).wait_recv()
    total_of(grad_r, 15).wait_recv()
    for g in range(num_groups):
        rows = slice(g * 64, (g + 1) * 64)
        res_out[rows] = jnp.concatenate([cut(res_r[band], g) for band in range(bands)], axis=1)
        grad_out[rows] = (
            jnp.concatenate([cut(grad_r[band], g) for band in range(bands)], axis=1)
            - tv_weight * spread[rows]
        )
    for buffer, phase in (
        (sky_s, 0), (tile_s, 1), (seen_s, 2), (noise_s, 3), (two_s, 4), (three_s, 5),
        (four_s, 6), (five_s, 7), (res_s, 8), (grad_s, 15),
    ):
        total_of(buffer, phase).wait_send()


def on_device(sky_image, observed, noise_weight, basis_tiles, intersection, counts, transfer):
    pool, tile_side = (basis_tiles.shape[0], basis_tiles.shape[1])
    shape = (lax.axis_size("sy"), lax.axis_size("sx"), *sky_image.shape, pool, tile_side)
    if shape + intersection.shape[2:] != (bands, band_size, 256, lanes, 4, lanes, 4):
        return generic_device(
            sky_image, observed, noise_weight, basis_tiles, intersection, counts, transfer
        )
    constants = tables()
    f32, bf16 = (jnp.float32, jnp.bfloat16)
    scalars = pl.BlockSpec(memory_space=pltpu.SMEM)

    def double(*dims, kind=f32):
        return [pltpu.VMEM(dims, kind)] * 2

    scratch = [
        pltpu.VMEM(transfer.shape, f32),
        *[pltpu.VMEM(table.shape, bf16) for table in constants],
        *double(bands, 72, lanes),
        *double(bands, 64, lanes),
        *double(bands, 64, lanes),
        *double(devices, 64, lanes, kind=bf16),
        *double(devices, 40, lanes, kind=jnp.int32),
        *double(devices, 16, lanes),
        *double(devices, 16, lanes),
        *double(devices, 40, lanes, kind=jnp.int32),
        *double(bands, 64, lanes),
        *double(bands, 64, lanes),
        *double(64, lanes),
        *double(8, lanes),
        *double(8, lanes),
        pltpu.VMEM((size, lanes), f32),
        pltpu.VMEM((size, 2 * lanes), bf16),
        pltpu.VMEM((512, size), bf16),
        pltpu.VMEM((128, size), bf16),
        pltpu.VMEM((2 * size, 2 * lanes), bf16),
        pltpu.VMEM((256, lanes), f32),
        pltpu.SemaphoreType.DMA((9,)),
        pltpu.SemaphoreType.DMA((16,)),
        pltpu.SemaphoreType.DMA((16,)),
    ]
    in_vmem = pl.BlockSpec(memory_space=pltpu.VMEM)
    outside = pl.BlockSpec(memory_space=pl.ANY)
    return pl.pallas_call(
        kernel,
        out_shape=[jax.ShapeDtypeStruct(sky_image.shape, f32)] * 2,
        in_specs=[in_vmem] * 4 + [scalars] * 2 + [outside] * 9,
        out_specs=[in_vmem] * 2,
        scratch_shapes=scratch,
        compiler_params=pltpu.CompilerParams(
            collective_id=0, has_side_effects=True, vmem_limit_bytes=56 * 1024 * 1024
        ),
        cost_estimate=pl.CostEstimate(
            flops=10_000_000_000, bytes_accessed=30_000_000, transcendentals=0
        ),
    )(
        sky_image, observed, noise_weight, basis_tiles, intersection, counts, transfer, *(jnp.asarray(table) for table in constants),
    )


def solution(mesh):
    placed = (
        P("sy", "sx"),
        P("sy", "sx"),
        P("sy", "sx"),
        P(("sy", "sx"), None, None),
        P(),
        P("sy", "sx"),
        P(None, None, ("sy", "sx"), None),
    )
    return jax.shard_map(
        on_device,
        mesh=mesh,
        in_specs=placed,
        out_specs=(P("sy", "sx"), P("sy", "sx")),
        check_vma=False,
    )
```

```python
import jax
import jax.numpy as jnp
import numpy as np
from jax import lax
from jax.experimental import pallas as pl
from jax.experimental.pallas import tpu as pltpu
from jax.sharding import PartitionSpec as P

radix = 128
highest = lax.Precision.HIGHEST
tv_weight = 0.5
smoothing = 0.25


def with_halo(block, sides, width):
    for axis, dim in sides:
        count = lax.axis_size(axis)
        forward = [(i, i + 1) for i in range(count - 1)]
        forward.append((count - 1, 0))
        backward = [(target, source) for source, target in forward]
        low = lax.ppermute(
            lax.slice_in_dim(block, block.shape[dim] - width, None, axis=dim), axis, forward
        )
        high = lax.ppermute(lax.slice_in_dim(block, 0, width, axis=dim), axis, backward)
        block = jnp.concatenate([low, block, high], axis=dim)
    return block


def circle(left_index, right_index, length, orient):
    product = left_index[:, None] * right_index[None, :] % length
    angles = product.astype(jnp.float32) * (2.0 * jnp.pi / length)
    return (jnp.cos(angles), orient * jnp.sin(angles))


def contract(pattern, operand, matrix):
    return jnp.einsum(pattern, operand, matrix, precision=highest)


def forward_last(stacked):
    num_parts, num_fields, num_lines, length = stacked.shape
    short_size = length // radix
    pieces = stacked.reshape(num_parts, num_fields, num_lines, short_size, radix)
    short_index = jnp.arange(short_size, dtype=jnp.int32)
    long_index = jnp.arange(radix, dtype=jnp.int32)
    cos_short, sin_short = circle(short_index, short_index, short_size, -1.0)
    cos_turn, sin_turn = circle(short_index, long_index, length, -1.0)
    cos_long, sin_long = circle(long_index, long_index, radix, -1.0)
    first_form = "fmba,bk->fmka"
    real_part = contract(first_form, pieces[0], cos_short)
    imag_part = contract(first_form, pieces[0], sin_short)
    if num_parts == 2:
        real_part = real_part - contract(first_form, pieces[1], sin_short)
        imag_part = imag_part + contract(first_form, pieces[1], cos_short)
    turned_real = real_part * cos_turn - imag_part * sin_turn
    turned_imag = real_part * sin_turn + imag_part * cos_turn
    second_form = "fmka,aj->fmkj"
    out_real = contract(second_form, turned_real, cos_long) - contract(
        second_form, turned_imag, sin_long
    )
    out_imag = contract(second_form, turned_real, sin_long) + contract(
        second_form, turned_imag, cos_long
    )
    return jnp.stack([out_real, out_imag]).reshape(2, num_fields, num_lines, length)


def inverse_last(stacked, real_only):
    num_fields, num_lines, length = (stacked.shape[1], stacked.shape[2], stacked.shape[3])
    short_size = length // radix
    pieces = stacked.reshape(2, num_fields, num_lines, short_size, radix)
    short_index = jnp.arange(short_size, dtype=jnp.int32)
    long_index = jnp.arange(radix, dtype=jnp.int32)
    cos_long, sin_long = circle(long_index, long_index, radix, 1.0)
    cos_turn, sin_turn = circle(short_index, long_index, length, 1.0)
    cos_short, sin_short = circle(short_index, short_index, short_size, 1.0)
    first_form = "fmkj,ja->fmka"
    real_part = contract(first_form, pieces[0], cos_long) - contract(
        first_form, pieces[1], sin_long
    )
    imag_part = contract(first_form, pieces[0], sin_long) + contract(
        first_form, pieces[1], cos_long
    )
    turned_real = real_part * cos_turn - imag_part * sin_turn
    turned_imag = real_part * sin_turn + imag_part * cos_turn
    second_form = "fmka,kb->fmba"
    out_real = contract(second_form, turned_real, cos_short) - contract(
        second_form, turned_imag, sin_short
    )
    if real_only:
        return out_real.reshape(1, num_fields, num_lines, length)
    out_imag = contract(second_form, turned_real, sin_short) + contract(
        second_form, turned_imag, cos_short
    )
    return jnp.stack([out_real, out_imag]).reshape(2, num_fields, num_lines, length)


def to_spectra(pixels):
    columns = lax.all_to_all(
        jnp.swapaxes(pixels, 2, 3), "sy", split_axis=2, concat_axis=3, tiled=True
    )
    along_y = forward_last(columns)
    blocks = lax.all_to_all(along_y, "sy", split_axis=3, concat_axis=2, tiled=True)
    lines = lax.all_to_all(
        jnp.swapaxes(blocks, 2, 3), "sx", split_axis=2, concat_axis=3, tiled=True
    )
    return forward_last(lines)


def from_spectra(spectrum, normalizer):
    along_x = inverse_last(spectrum, False)
    blocks = lax.all_to_all(along_x, "sx", split_axis=3, concat_axis=2, tiled=True)
    columns = lax.all_to_all(
        jnp.swapaxes(blocks, 2, 3), "sy", split_axis=2, concat_axis=3, tiled=True
    )
    values = inverse_last(columns, True) * normalizer
    pixel_blocks = lax.all_to_all(values, "sy", split_axis=3, concat_axis=2, tiled=True)
    return jnp.swapaxes(pixel_blocks, 2, 3)[0]


def generic_device(sky_image, observed, noise_weight, basis_tiles, intersection, counts, transfer):
    height, breadth = sky_image.shape
    pool_size, tile_side = (basis_tiles.shape[0], basis_tiles.shape[1])
    components = intersection.shape[2]
    tiles_down = height // tile_side
    tiles_across = breadth // tile_side
    band_size = lax.axis_size("sx")
    sky_row = lax.axis_index("sy")
    sky_column = lax.axis_index("sx")
    num_requests = tiles_down * tiles_across * components
    zero_index = jnp.zeros((), jnp.int32)
    own_lists = lax.dynamic_slice(
        intersection,
        (sky_row * tiles_down, sky_column * tiles_across, zero_index),
        (tiles_down, tiles_across, components),
    ).reshape(num_requests)
    band_start = sky_row * band_size * pool_size
    band_index = own_lists - band_start
    flat_tiles = basis_tiles.reshape(pool_size, tile_side * tile_side)
    piece = lax.all_gather(flat_tiles, "sx", axis=0, tiled=True)
    piece_count = piece.shape[0]
    hits = (band_index[:, None] == jnp.arange(piece_count, dtype=jnp.int32)[None, :]).astype(
        jnp.bfloat16
    )
    coefficient = jnp.dot(hits, piece, preferred_element_type=jnp.float32)
    in_use = (jnp.arange(components, dtype=jnp.int32)[None, None, :] < counts[:, :, None]).astype(
        jnp.float32
    )
    coef_maps = (
        coefficient.reshape(tiles_down, tiles_across, components, tile_side, tile_side)
        * in_use[:, :, :, None, None]
    )
    weights = coef_maps.transpose(2, 0, 3, 1, 4).reshape(components, height, breadth)
    normalizer = 1.0 / (transfer.shape[2] * lax.axis_size("sy") * band_size * transfer.shape[3])
    spectra = to_spectra((weights * sky_image[None])[None])
    trans_real = transfer[:, 0]
    trans_imag = transfer[:, 1]
    model_real = jnp.sum(spectra[0] * trans_real - spectra[1] * trans_imag, axis=0)
    model_imag = jnp.sum(spectra[0] * trans_imag + spectra[1] * trans_real, axis=0)
    blurred = from_spectra(jnp.stack([model_real, model_imag])[:, None], normalizer)[0]
    residual = noise_weight * (blurred - observed)
    back_spectrum = to_spectra(residual[None, None])
    pull_real = back_spectrum[0] * trans_real + back_spectrum[1] * trans_imag
    pull_imag = back_spectrum[1] * trans_real - back_spectrum[0] * trans_imag
    pulled = from_spectra(jnp.stack([pull_real, pull_imag]), normalizer)
    data_grad = jnp.sum(weights * pulled, axis=0)
    framed = with_halo(sky_image, (("sy", 0), ("sx", 1)), 1)
    step_x = framed[:-1, 1:] - framed[:-1, :-1]
    step_y = framed[1:, :-1] - framed[:-1, :-1]
    magnitude = jnp.sqrt(step_x * step_x + step_y * step_y + smoothing)
    flow_x = step_x / magnitude
    flow_y = step_y / magnitude
    spread = flow_x[1:, 1:] - flow_x[1:, :-1] + flow_y[1:, 1:] - flow_y[:-1, 1:]
    gradient = data_grad - tv_weight * spread
    return (residual, gradient)


lanes = 128
group = 32
num_groups = 4
bands = 4
band_size = 8
devices = 32
size = 1024
MESH = pl.DeviceIdType.MESH


def split_table(values):
    high = values.astype(jnp.bfloat16)
    return high, (values - high.astype(np.float64)).astype(jnp.bfloat16)


def tables():
    spot = np.arange(size)
    owner, column = (spot // group, spot % group)
    pixel = (owner % band_size) * lanes + (owner // band_size) * group + column
    frequency = (size // radix) * (spot % radix) + spot // radix
    angle = (frequency[:, None] * spot[None, :] % size) * (2.0 * np.pi / size)
    parts = np.stack([np.cos(angle), -np.sin(angle)]).reshape(2, devices, group, size)
    along_y = parts.transpose(1, 0, 2, 3).reshape(2 * size, size)
    angle = (pixel[:, None] * frequency[None, :] % size) * (2.0 * np.pi / size)
    cos_high, cos_low = split_table(np.cos(angle))
    sin_high, sin_low = split_table(np.sin(angle))
    return (
        *split_table(along_y),
        cos_high,
        sin_high,
        cos_low,
        sin_low,
        *split_table(np.ascontiguousarray(along_y.T)),
    )


def split(values):
    high = values.astype(jnp.bfloat16)
    return high, (values - high.astype(jnp.float32)).astype(jnp.bfloat16)


def mul(left, right):
    return jnp.dot(left, right, preferred_element_type=jnp.float32)


def mul_t(left, right):
    return lax.dot_general(
        left, right, (((1,), (1,)), ((), ())), preferred_element_type=jnp.float32
    )


def cut(values, index):
    return values[:, index * group : (index + 1) * group]


def lane_groups(rows):
    return lax.broadcasted_iota(jnp.int32, (rows, lanes), 1) // group


def pick_groups(pieces):
    where = lane_groups(pieces[0].shape[0])
    out = pieces[0]
    for index in range(1, num_groups):
        out = jnp.where(where == index, pieces[index], out)
    return out


def fold(values):
    values = values + pltpu.roll(values, 64, 1)
    return values + pltpu.roll(values, 32, 1)


def encode(real, imag):
    largest = jnp.max(jnp.maximum(jnp.abs(real), jnp.abs(imag)), axis=0, keepdims=True)
    level = jnp.ceil(jnp.log2(jnp.maximum(largest, 1e-30)) * 256.0 + 0.01)
    factor = 32760.0 * jnp.exp2(level * (-1.0 / 256.0))
    high = jnp.floor(real * factor + 0.5).astype(jnp.int32)
    low = jnp.floor(imag * factor + 0.5).astype(jnp.int32)
    return high * 65536 + (low + 32768), level.astype(jnp.int32)


def decode(packed, level):
    factor = jnp.exp2(level.astype(jnp.float32) * (1.0 / 256.0)) * (1.0 / 32760.0)
    real = (packed >> 16).astype(jnp.float32) * factor
    imag = ((packed & 65535) - 32768).astype(jnp.float32) * factor
    return real, imag


def pull(total, sky, left, right, below, above, below_left, above_right):
    rows = sky.shape[0]
    lane = lax.broadcasted_iota(jnp.int32, sky.shape, 1)
    row = lax.broadcasted_iota(jnp.int32, sky.shape, 0)

    def flows(step_x, step_y):
        magnitude = jnp.sqrt(step_x * step_x + step_y * step_y + smoothing)
        return step_x / magnitude, step_y / magnitude

    next_x = jnp.where(lane == lanes - 1, right, pltpu.roll(sky, lanes - 1, 1))
    next_y = jnp.where(row == rows - 1, below, pltpu.roll(sky, rows - 1, 0))
    flow_x, flow_y = flows(next_x - sky, next_y - sky)
    left_next = jnp.where(row == rows - 1, below_left, pltpu.roll(left, rows - 1, 0))
    side_x, _ = flows(sky - left, left_next - left)
    side_x = side_x[:, 0:1]
    above_next = jnp.where(lane[0:8] == lanes - 1, above_right, pltpu.roll(above, lanes - 1, 1))
    _, top_y = flows(above_next - above, sky[0:1] - above)
    before_x = jnp.where(lane == 0, side_x, pltpu.roll(flow_x, 1, 1))
    before_y = jnp.where(row == 0, top_y[7:8], pltpu.roll(flow_y, 1, 0))
    total[...] = flow_x - before_x + flow_y - before_y


def kernel(
    sky, seen, noise, basis, lists, counts,
    trans_hbm, fyh_hbm, fyl_hbm, cxh_hbm, sxh_hbm, cxl_hbm, sxl_hbm, gh_hbm, gl_hbm,
    res_out, grad_out,
    trans, fyh, fyl, cxh, sxh, cxl, sxl, gh, gl,
    sky_s, sky_r, seen_s, seen_r, noise_s, noise_r, tile_s, tile_r,
    two_s, two_r, three_s, three_r, four_s, four_r, five_s, five_r,
    res_s, res_r, grad_s, grad_r,
    halo_left, halo_right, halo_below, halo_above, halo_bl, halo_ar,
    weights, fields, wide, narrow, tall, spread, spectra, pulled,
    load_sem, send_sem, recv_sem,
):
    my_y, my_x = (lax.axis_index("sy"), lax.axis_index("sx"))
    me = my_y * band_size + my_x
    barrier = pltpu.get_barrier_semaphore()

    def greet(step, carry):
        other = lax.rem(me + step, devices)
        pl.semaphore_signal(
            barrier, inc=1, device_id=(other // band_size, lax.rem(other, band_size)),
            device_id_type=MESH,
        )
        return carry

    lax.fori_loop(1, devices, greet, 0)
    loads = []
    pairs = (
        (fyh_hbm, fyh), (fyl_hbm, fyl), (cxh_hbm, cxh), (sxh_hbm, sxh), (cxl_hbm, cxl),
        (sxl_hbm, sxl), (trans_hbm, trans), (gh_hbm, gh), (gl_hbm, gl),
    )
    for index, (source, target) in enumerate(pairs):
        loads.append(pltpu.make_async_copy(source, target, load_sem.at[index]))
        loads[-1].start()

    def send(source, target, phase, where, arrival=None):
        arrival = phase if arrival is None else arrival
        pltpu.make_async_remote_copy(
            src_ref=source, dst_ref=target, send_sem=send_sem.at[phase],
            recv_sem=recv_sem.at[arrival], device_id=where, device_id_type=MESH,
        ).start()

    def total_of(buffer, phase, count=None):
        part = buffer.at[pl.ds(0, buffer.shape[0] - 1 if count is None else count)]
        return pltpu.make_async_remote_copy(
            src_ref=part, dst_ref=part, send_sem=send_sem.at[phase],
            recv_sem=recv_sem.at[phase], device_id=(lax.rem(my_y + 1, bands), my_x),
            device_id_type=MESH,
        )

    def arrived(buffer, first, plane):
        @pl.when(plane != my_y)
        def _():
            total_of(buffer, first + plane, band_size).wait_recv()

        @pl.when(plane == my_y)
        def _():
            total_of(buffer, first + plane, band_size - 1).wait_recv()

    def to_all(source, target, phase, other, arrival=None):
        @pl.when(other != me)
        def _():
            send(
                source.at[other], target.at[me], phase,
                (other // band_size, lax.rem(other, band_size)), arrival,
            )

        @pl.when(other == me)
        def _():
            target[me] = source[me]

    def to_band(source, target, phase, other):
        @pl.when(other != my_y)
        def _():
            send(source.at[other], target.at[my_y], phase, (other, my_x))

        @pl.when(other == my_y)
        def _():
            target[my_y] = source[my_y]

    def pack(block, other):
        return jnp.concatenate(
            [cut(block[g * 64 : (g + 1) * 64], other) for g in range(num_groups)], axis=1
        )

    row = lax.broadcasted_iota(jnp.int32, (8, lanes), 0)
    mask = jnp.where(row % 4 < jnp.where(row < 4, counts[0, 0], counts[1, 0]), 1.0, 0.0)
    slot_lane = lane_groups(64) % 2
    for other in range(bands):
        sky_s[other, 0:64] = pack(sky[...], other)
        sky_s[other, 64:72] = mask
    pl.semaphore_wait(barrier, devices - 1)
    for step in range(bands):
        to_band(sky_s, sky_r, 0, lax.rem(my_y + 1 + step, bands))

    for other in range(bands):
        packs = []
        for t in range(4):
            part = cut(basis[t].astype(jnp.float32), other)
            packs.append(
                jnp.concatenate([part[0:64], part[0:64], part[64:128], part[64:128]], axis=1)
            )

        def choose(column, carry):
            first, second, seen_before = (-1, -1, 0)
            for e in range(8):
                local = lists[my_y * 2 + e // 4, column, e % 4] - me * 4
                hit = (local >= 0) & (local < 4)
                first = jnp.where(hit & (seen_before == 0), local, first)
                second = jnp.where(hit & (seen_before == 1), local, second)
                seen_before = seen_before + jnp.where(hit, 1, 0)
            wanted = jnp.where(slot_lane == 0, first, second)
            acc = jnp.where(wanted == 0, packs[0], 0.0)
            for t in range(1, 4):
                acc = jnp.where(wanted == t, packs[t], acc)
            tile_s[other * band_size + column] = acc.astype(jnp.bfloat16)
            return carry

        lax.fori_loop(0, band_size, choose, 0)

    def send_tiles(step, carry):
        plane = lax.rem(my_y + 1 + step // band_size, bands)
        to_all(tile_s, tile_r, 1, plane * band_size + lax.rem(my_x + step, band_size))
        return carry

    lax.fori_loop(0, devices, send_tiles, 0)

    for other in range(bands):
        seen_s[other] = pack(seen[...], other)
        noise_s[other] = pack(noise[...], other)
    for step in range(bands):
        to_band(seen_s, seen_r, 2, lax.rem(my_y + 1 + step, bands))
        to_band(noise_s, noise_r, 3, lax.rem(my_y + 1 + step, bands))
    up, down = (lax.rem(my_y + bands - 1, bands), lax.rem(my_y + 1, bands))
    west, east = (lax.rem(my_x + band_size - 1, band_size), lax.rem(my_x + 1, band_size))
    first, last = (sky.at[pl.ds(0, 8)], sky.at[pl.ds(248, 8)])
    halos = (
        (sky_s.at[0, pl.ds(0, 64)], halo_right, (my_y, west)),
        (sky_s.at[bands - 1, pl.ds(0, 64)], halo_left, (my_y, east)),
        (first, halo_below, (up, my_x)),
        (first, halo_bl, (up, east)),
        (last, halo_above, (down, my_x)),
        (last, halo_ar, (down, west)),
    )
    for index, (source, target, where) in enumerate(halos):
        send(source, target, 9 + index, where)

    total_of(sky_r, 0).wait_recv()
    total_of(tile_r, 1).wait_recv()

    def weigh(band, carry):
        parts = []
        tiles = [tile_r[band * band_size + h].astype(jnp.float32) for h in range(band_size)]
        holders = [
            lists[band * 2 + e // 4, my_x, e % 4] // 4 - band * band_size for e in range(8)
        ]
        for e in range(8):
            slot = 0
            for earlier in range(e):
                slot = slot + jnp.where(holders[earlier] == holders[e], 1, 0)
            place = holders[e] * 2 + slot
            acc = jnp.zeros((64, lanes), jnp.float32)
            for h in range(band_size):
                acc = jnp.where(slot_lane + 2 * h == place, tiles[h], acc)
            acc = (acc + pltpu.roll(acc, 96, 1)) * sky_r[band, 64 + e : 65 + e]
            parts.append(acc)
        for g in range(num_groups):
            down_tile, half = (g // 2, g % 2)
            block = jnp.concatenate(
                [cut(parts[down_tile * 4 + k], 2 * half) for k in range(4)], axis=1
            )
            rows = pl.ds(pl.multiple_of(band * 256 + g * 64, 64), 64)
            weights[rows] = block
            high, low = split(
                block * jnp.concatenate([cut(sky_r[band, 0:64], g)] * num_groups, axis=1)
            )
            fields[rows, 0:128] = high
            fields[rows, 128:256] = low
        return carry

    lax.fori_loop(0, bands, weigh, 0)
    loads[0].wait()
    loads[1].wait()

    def along_y(step):
        part = lax.rem(my_y + 1 + step // 2, bands) * 2 + lax.rem(step + my_x, 2)
        rows = pl.ds(pl.multiple_of(part * 256, 256), 256)
        both = mul(fyh[rows], fields[...])
        return part, both[:, 0:128] + both[:, 128:256] + mul(fyl[rows], fields[:, 0:128])

    def forward_y(step, carry):
        part, out = along_y(step)
        for j in range(4):
            other = part * 4 + j
            packed, level = encode(out[j * 64 : j * 64 + 32], out[j * 64 + 32 : j * 64 + 64])
            two_s[other, 0:32] = packed
            two_s[other, 32:40] = jnp.broadcast_to(level, (8, lanes))
        for j in range(4):
            to_all(two_s, two_r, 4, part * 4 + lax.rem(my_x + j, 4), 16 + my_y)
        return carry

    lax.fori_loop(0, 8, forward_y, 0)

    for index, (source, target, where) in enumerate(halos):
        pltpu.make_async_remote_copy(
            src_ref=source, dst_ref=target, send_sem=send_sem.at[9 + index],
            recv_sem=recv_sem.at[9 + index], device_id=where, device_id_type=MESH,
        ).wait()

    def side(buffer, lane):
        return jnp.concatenate(
            [
                buffer[:, g * group + lane : g * group + lane + 1] + jnp.zeros((64, lanes))
                for g in range(num_groups)
            ],
            axis=0,
        )

    pull(
        spread, sky[...], side(halo_left, group - 1), side(halo_right, 0), halo_below[0:1],
        halo_above[...], halo_bl[0:1, 127:128], halo_ar[7:8, 0:1],
    )

    for index in range(2, 7):
        loads[index].wait()

    def gather_two(g):
        at = pl.ds(pl.multiple_of(g * 128, 128), 128)
        parts = [decode(two_r[4 * g + j, 0:32], two_r[4 * g + j, 32:33]) for j in range(4)]
        for c in range(2):
            blocks = [part[c] for part in parts]
            for k in range(4):
                high, low = split(jnp.concatenate([cut(block, k) for block in blocks], axis=1))
                row = c * 128 + k * 32
                wide[row : row + 32, at] = high
                wide[256 + row : 288 + row, at] = low

    def along_x(buffer, half, at, inner):
        cos_part = mul(buffer[:, inner], cxh[inner, at])
        sin_part = mul(buffer[:, inner], sxh[inner, at])
        cos_part = cos_part[0:half] + cos_part[half:] + mul(buffer[0:half, inner], cxl[inner, at])
        sin_part = sin_part[0:half] + sin_part[half:] + mul(buffer[0:half, inner], sxl[inner, at])
        q = half // 2
        return cos_part[0:q] + sin_part[q:half], cos_part[q:half] - sin_part[0:q]

    spectra[...] = jnp.zeros_like(spectra)

    def add_plane(step, carry):
        plane = lax.rem(my_y + bands - 1 - step, bands)
        arrived(two_r, 16, plane)
        gather_two(plane * 2)
        gather_two(plane * 2 + 1)
        inner = pl.ds(pl.multiple_of(plane * 256, 256), 256)
        for n in range(4):
            at = slice(n * 256, (n + 1) * 256)
            real, imag = along_x(wide, 256, at, inner)
            spectra[0, :, at] += real
            spectra[1, :, at] += imag
        return carry

    lax.fori_loop(0, bands, add_plane, 0)

    def back_x(buffer, half, rows):
        cos_part = mul_t(buffer[...], cxh[rows])
        sin_part = mul_t(buffer[...], sxh[rows])
        cos_part = cos_part[0:half] + cos_part[half:] + mul_t(buffer[0:half], cxl[rows])
        sin_part = sin_part[0:half] + sin_part[half:] + mul_t(buffer[0:half], sxl[rows])
        q = half // 2
        return cos_part[0:q] - sin_part[q:half], cos_part[q:half] + sin_part[0:q]

    def model(step, carry):
        at = pl.ds(pl.multiple_of(step * 256, 256), 256)
        real, imag = (spectra[0, :, at], spectra[1, :, at])
        sum_real, sum_imag = (0.0, 0.0)
        for k in range(4):
            rows = slice(k * 32, (k + 1) * 32)
            trans_real, trans_imag = (trans[k, 0, :, at], trans[k, 1, :, at])
            sum_real = sum_real + real[rows] * trans_real - imag[rows] * trans_imag
            sum_imag = sum_imag + real[rows] * trans_imag + imag[rows] * trans_real
        for c, part in enumerate((sum_real, sum_imag)):
            high, low = split(part)
            narrow[c * 32 : (c + 1) * 32, at] = high
            narrow[64 + c * 32 : 96 + c * 32, at] = low
        return carry

    lax.fori_loop(0, 4, model, 0)

    def back_three(step, carry):
        part = lax.rem(me // 8 + 1 + step, 4)
        rows = pl.ds(pl.multiple_of(part * 256, 256), 256)
        real, imag = back_x(narrow, 64, rows)
        for j in range(8):
            other = part * 8 + j
            three_s[other] = jnp.concatenate(
                [cut(real[0:16], j), cut(imag[0:16], j), cut(real[16:32], j), cut(imag[16:32], j)],
                axis=1,
            )
        for j in range(8):
            to_all(three_s, three_r, 5, part * 8 + lax.rem(my_x + j, 8))
        return carry

    lax.fori_loop(0, 4, back_three, 0)
    loads[7].wait()
    loads[8].wait()
    total_of(seen_r, 2).wait_recv()
    total_of(noise_r, 3).wait_recv()
    total_of(three_r, 5).wait_recv()

    def spread_three(source, carry):
        block = three_r[source]
        where = lane_groups(16)
        for c in range(2):
            for h in range(2):
                high, low = split(jnp.where(where == h * 2 + c, block, 0.0))
                rows = pl.ds(pl.multiple_of(source * 64 + c * 32 + h * 16, 16), 16)
                tall[rows, 0:128] = high
                tall[rows, 128:256] = low
        return carry

    lax.fori_loop(0, devices, spread_three, 0)
    normalizer = 1.0 / (size * size)

    def back_y(rows):
        both = mul(gh[rows], tall[...])
        out = both[:, 0:128] + both[:, 128:256] + mul(gl[rows], tall[:, 0:128])
        return out * normalizer

    def residual(step, carry):
        band = lax.rem(my_y + 1 + step, bands)
        rows = pl.ds(pl.multiple_of(band * 256, 256), 256)
        out = fold(back_y(rows))
        blurred = pick_groups([out[g * 64 : (g + 1) * 64] for g in range(num_groups)])
        left_over = noise_r[band] * (blurred - seen_r[band])
        res_s[band] = left_over
        for g in range(num_groups):
            high, low = split(jnp.concatenate([cut(left_over, g)] * num_groups, axis=1))
            rows = pl.ds(pl.multiple_of(band * 256 + g * 64, 64), 64)
            fields[rows, 0:128] = high
            fields[rows, 128:256] = low
        return carry

    lax.fori_loop(0, bands, residual, 0)

    def forward_four(step, carry):
        part, out = along_y(step)
        for j in range(4):
            other = part * 4 + j
            pieces = []
            for h in range(2):
                for c in range(2):
                    row = j * 64 + c * 32 + h * 16
                    pieces.append(out[row : row + 16])
            four_s[other] = pick_groups(pieces)
        for j in range(4):
            to_all(four_s, four_r, 6, part * 4 + lax.rem(my_x + j, 4))
        return carry

    lax.fori_loop(0, 8, forward_four, 0)
    for other in range(bands):
        to_band(res_s, res_r, 8, other)
    total_of(four_r, 6).wait_recv()

    def gather_four(g, carry):
        at = pl.ds(pl.multiple_of(g * 128, 128), 128)
        blocks = [four_r[4 * g + j] for j in range(4)]
        for c in range(2):
            for h in range(2):
                high, low = split(
                    jnp.concatenate([cut(block, h * 2 + c) for block in blocks], axis=1)
                )
                row = c * 32 + h * 16
                narrow[row : row + 16, at] = high
                narrow[64 + row : 80 + row, at] = low
        return carry

    lax.fori_loop(0, 8, gather_four, 0)

    def adjoint(step, carry):
        at = pl.ds(pl.multiple_of(step * 256, 256), 256)
        real, imag = along_x(narrow, 64, at, slice(None))
        for k in range(4):
            trans_real, trans_imag = (trans[k, 0, :, at], trans[k, 1, :, at])
            both = (real * trans_real + imag * trans_imag, imag * trans_real - real * trans_imag)
            for c in range(2):
                high, low = split(both[c])
                row = c * 128 + k * 32
                wide[row : row + 32, at] = high
                wide[256 + row : 288 + row, at] = low
        return carry

    lax.fori_loop(0, 4, adjoint, 0)

    def back_five(step, carry):
        part = lax.rem(me // 8 + 1 + step, 4)
        rows = pl.ds(pl.multiple_of(part * 256, 256), 256)
        both = back_x(wide, 256, rows)
        for j in range(8):
            other = part * 8 + j
            real, imag = [
                jnp.concatenate([cut(part[k * 32 : (k + 1) * 32], j) for k in range(4)], axis=1)
                for part in both
            ]
            packed, level = encode(real, imag)
            five_s[other, 0:32] = packed
            five_s[other, 32:40] = jnp.broadcast_to(level, (8, lanes))
        for j in range(8):
            to_all(five_s, five_r, 7, part * 8 + lax.rem(my_x + j, 8), 20 + my_y)
        return carry

    lax.fori_loop(0, 4, back_five, 0)
    pulled[...] = jnp.zeros_like(pulled)

    def split_five(source, carry):
        parts = decode(five_r[source, 0:32], five_r[source, 32:33])
        for c in range(2):
            high, low = split(parts[c])
            rows = pl.ds(pl.multiple_of(source * 64 + c * 32, 32), 32)
            tall[rows, 0:128] = high
            tall[rows, 128:256] = low
        return carry

    def add_five(step, carry):
        plane = lax.rem(my_y + bands - 1 - step, bands)
        arrived(five_r, 20, plane)
        lax.fori_loop(plane * band_size, (plane + 1) * band_size, split_five, 0)
        inner = pl.ds(pl.multiple_of(plane * 512, 512), 512)
        for band in range(bands):
            rows = slice(band * 256, (band + 1) * 256)
            both = mul(gh[rows, inner], tall[inner])
            both = both[:, 0:128] + both[:, 128:256] + mul(gl[rows, inner], tall[inner, 0:128])
            pulled[rows] += both
        return carry

    lax.fori_loop(0, bands, add_five, 0)

    def finish(step, carry):
        band = lax.rem(my_y + 1 + step, bands)
        rows = pl.ds(pl.multiple_of(band * 256, 256), 256)
        out = fold(pulled[rows] * weights[rows] * normalizer)
        grad_s[band] = pick_groups([out[g * 64 : (g + 1) * 64] for g in range(num_groups)])
        to_band(grad_s, grad_r, 15, band)
        return carry

    lax.fori_loop(0, bands, finish, 0)
    total_of(res_r, 8).wait_recv()
    total_of(grad_r, 15).wait_recv()
    for g in range(num_groups):
        rows = slice(g * 64, (g + 1) * 64)
        res_out[rows] = jnp.concatenate([cut(res_r[band], g) for band in range(bands)], axis=1)
        grad_out[rows] = (
            jnp.concatenate([cut(grad_r[band], g) for band in range(bands)], axis=1)
            - tv_weight * spread[rows]
        )
    for buffer, phase in (
        (sky_s, 0), (tile_s, 1), (seen_s, 2), (noise_s, 3), (two_s, 4), (three_s, 5),
        (four_s, 6), (five_s, 7), (res_s, 8), (grad_s, 15),
    ):
        total_of(buffer, phase).wait_send()


def on_device(sky_image, observed, noise_weight, basis_tiles, intersection, counts, transfer):
    pool, tile_side = (basis_tiles.shape[0], basis_tiles.shape[1])
    shape = (lax.axis_size("sy"), lax.axis_size("sx"), *sky_image.shape, pool, tile_side)
    if shape + intersection.shape[2:] != (bands, band_size, 256, lanes, 4, lanes, 4):
        return generic_device(
            sky_image, observed, noise_weight, basis_tiles, intersection, counts, transfer
        )
    constants = tables()
    f32, bf16 = (jnp.float32, jnp.bfloat16)
    scalars = pl.BlockSpec(memory_space=pltpu.SMEM)

    def double(*dims, kind=f32):
        return [pltpu.VMEM(dims, kind)] * 2

    scratch = [
        pltpu.VMEM(transfer.shape, f32),
        *[pltpu.VMEM(table.shape, bf16) for table in constants],
        *double(bands, 72, lanes),
        *double(bands, 64, lanes),
        *double(bands, 64, lanes),
        *double(devices, 64, lanes, kind=bf16),
        *double(devices, 40, lanes, kind=jnp.int32),
        *double(devices, 16, lanes),
        *double(devices, 16, lanes),
        *double(devices, 40, lanes, kind=jnp.int32),
        *double(bands, 64, lanes),
        *double(bands, 64, lanes),
        *double(64, lanes),
        *double(8, lanes),
        *double(8, lanes),
        pltpu.VMEM((size, lanes), f32),
        pltpu.VMEM((size, 2 * lanes), bf16),
        pltpu.VMEM((512, size), bf16),
        pltpu.VMEM((128, size), bf16),
        pltpu.VMEM((2 * size, 2 * lanes), bf16),
        pltpu.VMEM((256, lanes), f32),
        pltpu.VMEM((2, lanes, size), f32),
        pltpu.VMEM((size, lanes), f32),
        pltpu.SemaphoreType.DMA((9,)),
        pltpu.SemaphoreType.DMA((16,)),
        pltpu.SemaphoreType.DMA((24,)),
    ]
    in_vmem = pl.BlockSpec(memory_space=pltpu.VMEM)
    outside = pl.BlockSpec(memory_space=pl.ANY)
    return pl.pallas_call(
        kernel,
        out_shape=[jax.ShapeDtypeStruct(sky_image.shape, f32)] * 2,
        in_specs=[in_vmem] * 4 + [scalars] * 2 + [outside] * 9,
        out_specs=[in_vmem] * 2,
        scratch_shapes=scratch,
        compiler_params=pltpu.CompilerParams(
            collective_id=0, has_side_effects=True, vmem_limit_bytes=56 * 1024 * 1024
        ),
        cost_estimate=pl.CostEstimate(
            flops=10_000_000_000, bytes_accessed=30_000_000, transcendentals=0
        ),
    )(
        sky_image, observed, noise_weight, basis_tiles, intersection, counts, transfer, *(jnp.asarray(table) for table in constants),
    )


def solution(mesh):
    placed = (
        P("sy", "sx"),
        P("sy", "sx"),
        P("sy", "sx"),
        P(("sy", "sx"), None, None),
        P(),
        P("sy", "sx"),
        P(None, None, ("sy", "sx"), None),
    )
    return jax.shard_map(
        on_device,
        mesh=mesh,
        in_specs=placed,
        out_specs=(P("sy", "sx"), P("sy", "sx")),
        check_vma=False,
    )
```

```python
import jax
import jax.numpy as jnp
import numpy as np
from jax import lax
from jax.experimental import pallas as pl
from jax.experimental.pallas import tpu as pltpu
from jax.sharding import PartitionSpec as P

radix = 128
highest = lax.Precision.HIGHEST
tv_weight = 0.5
smoothing = 0.25


def with_halo(block, sides, width):
    for axis, dim in sides:
        count = lax.axis_size(axis)
        forward = [(i, i + 1) for i in range(count - 1)]
        forward.append((count - 1, 0))
        backward = [(target, source) for source, target in forward]
        low = lax.ppermute(
            lax.slice_in_dim(block, block.shape[dim] - width, None, axis=dim), axis, forward
        )
        high = lax.ppermute(lax.slice_in_dim(block, 0, width, axis=dim), axis, backward)
        block = jnp.concatenate([low, block, high], axis=dim)
    return block


def circle(left_index, right_index, length, orient):
    product = left_index[:, None] * right_index[None, :] % length
    angles = product.astype(jnp.float32) * (2.0 * jnp.pi / length)
    return (jnp.cos(angles), orient * jnp.sin(angles))


def contract(pattern, operand, matrix):
    return jnp.einsum(pattern, operand, matrix, precision=highest)


def forward_last(stacked):
    num_parts, num_fields, num_lines, length = stacked.shape
    short_size = length // radix
    pieces = stacked.reshape(num_parts, num_fields, num_lines, short_size, radix)
    short_index = jnp.arange(short_size, dtype=jnp.int32)
    long_index = jnp.arange(radix, dtype=jnp.int32)
    cos_short, sin_short = circle(short_index, short_index, short_size, -1.0)
    cos_turn, sin_turn = circle(short_index, long_index, length, -1.0)
    cos_long, sin_long = circle(long_index, long_index, radix, -1.0)
    first_form = "fmba,bk->fmka"
    real_part = contract(first_form, pieces[0], cos_short)
    imag_part = contract(first_form, pieces[0], sin_short)
    if num_parts == 2:
        real_part = real_part - contract(first_form, pieces[1], sin_short)
        imag_part = imag_part + contract(first_form, pieces[1], cos_short)
    turned_real = real_part * cos_turn - imag_part * sin_turn
    turned_imag = real_part * sin_turn + imag_part * cos_turn
    second_form = "fmka,aj->fmkj"
    out_real = contract(second_form, turned_real, cos_long) - contract(
        second_form, turned_imag, sin_long
    )
    out_imag = contract(second_form, turned_real, sin_long) + contract(
        second_form, turned_imag, cos_long
    )
    return jnp.stack([out_real, out_imag]).reshape(2, num_fields, num_lines, length)


def inverse_last(stacked, real_only):
    num_fields, num_lines, length = (stacked.shape[1], stacked.shape[2], stacked.shape[3])
    short_size = length // radix
    pieces = stacked.reshape(2, num_fields, num_lines, short_size, radix)
    short_index = jnp.arange(short_size, dtype=jnp.int32)
    long_index = jnp.arange(radix, dtype=jnp.int32)
    cos_long, sin_long = circle(long_index, long_index, radix, 1.0)
    cos_turn, sin_turn = circle(short_index, long_index, length, 1.0)
    cos_short, sin_short = circle(short_index, short_index, short_size, 1.0)
    first_form = "fmkj,ja->fmka"
    real_part = contract(first_form, pieces[0], cos_long) - contract(
        first_form, pieces[1], sin_long
    )
    imag_part = contract(first_form, pieces[0], sin_long) + contract(
        first_form, pieces[1], cos_long
    )
    turned_real = real_part * cos_turn - imag_part * sin_turn
    turned_imag = real_part * sin_turn + imag_part * cos_turn
    second_form = "fmka,kb->fmba"
    out_real = contract(second_form, turned_real, cos_short) - contract(
        second_form, turned_imag, sin_short
    )
    if real_only:
        return out_real.reshape(1, num_fields, num_lines, length)
    out_imag = contract(second_form, turned_real, sin_short) + contract(
        second_form, turned_imag, cos_short
    )
    return jnp.stack([out_real, out_imag]).reshape(2, num_fields, num_lines, length)


def to_spectra(pixels):
    columns = lax.all_to_all(
        jnp.swapaxes(pixels, 2, 3), "sy", split_axis=2, concat_axis=3, tiled=True
    )
    along_y = forward_last(columns)
    blocks = lax.all_to_all(along_y, "sy", split_axis=3, concat_axis=2, tiled=True)
    lines = lax.all_to_all(
        jnp.swapaxes(blocks, 2, 3), "sx", split_axis=2, concat_axis=3, tiled=True
    )
    return forward_last(lines)


def from_spectra(spectrum, normalizer):
    along_x = inverse_last(spectrum, False)
    blocks = lax.all_to_all(along_x, "sx", split_axis=3, concat_axis=2, tiled=True)
    columns = lax.all_to_all(
        jnp.swapaxes(blocks, 2, 3), "sy", split_axis=2, concat_axis=3, tiled=True
    )
    values = inverse_last(columns, True) * normalizer
    pixel_blocks = lax.all_to_all(values, "sy", split_axis=3, concat_axis=2, tiled=True)
    return jnp.swapaxes(pixel_blocks, 2, 3)[0]


def generic_device(sky_image, observed, noise_weight, basis_tiles, intersection, counts, transfer):
    height, breadth = sky_image.shape
    pool_size, tile_side = (basis_tiles.shape[0], basis_tiles.shape[1])
    components = intersection.shape[2]
    tiles_down = height // tile_side
    tiles_across = breadth // tile_side
    band_size = lax.axis_size("sx")
    sky_row = lax.axis_index("sy")
    sky_column = lax.axis_index("sx")
    num_requests = tiles_down * tiles_across * components
    zero_index = jnp.zeros((), jnp.int32)
    own_lists = lax.dynamic_slice(
        intersection,
        (sky_row * tiles_down, sky_column * tiles_across, zero_index),
        (tiles_down, tiles_across, components),
    ).reshape(num_requests)
    band_start = sky_row * band_size * pool_size
    band_index = own_lists - band_start
    flat_tiles = basis_tiles.reshape(pool_size, tile_side * tile_side)
    piece = lax.all_gather(flat_tiles, "sx", axis=0, tiled=True)
    piece_count = piece.shape[0]
    hits = (band_index[:, None] == jnp.arange(piece_count, dtype=jnp.int32)[None, :]).astype(
        jnp.bfloat16
    )
    coefficient = jnp.dot(hits, piece, preferred_element_type=jnp.float32)
    in_use = (jnp.arange(components, dtype=jnp.int32)[None, None, :] < counts[:, :, None]).astype(
        jnp.float32
    )
    coef_maps = (
        coefficient.reshape(tiles_down, tiles_across, components, tile_side, tile_side)
        * in_use[:, :, :, None, None]
    )
    weights = coef_maps.transpose(2, 0, 3, 1, 4).reshape(components, height, breadth)
    normalizer = 1.0 / (transfer.shape[2] * lax.axis_size("sy") * band_size * transfer.shape[3])
    spectra = to_spectra((weights * sky_image[None])[None])
    trans_real = transfer[:, 0]
    trans_imag = transfer[:, 1]
    model_real = jnp.sum(spectra[0] * trans_real - spectra[1] * trans_imag, axis=0)
    model_imag = jnp.sum(spectra[0] * trans_imag + spectra[1] * trans_real, axis=0)
    blurred = from_spectra(jnp.stack([model_real, model_imag])[:, None], normalizer)[0]
    residual = noise_weight * (blurred - observed)
    back_spectrum = to_spectra(residual[None, None])
    pull_real = back_spectrum[0] * trans_real + back_spectrum[1] * trans_imag
    pull_imag = back_spectrum[1] * trans_real - back_spectrum[0] * trans_imag
    pulled = from_spectra(jnp.stack([pull_real, pull_imag]), normalizer)
    data_grad = jnp.sum(weights * pulled, axis=0)
    framed = with_halo(sky_image, (("sy", 0), ("sx", 1)), 1)
    step_x = framed[:-1, 1:] - framed[:-1, :-1]
    step_y = framed[1:, :-1] - framed[:-1, :-1]
    magnitude = jnp.sqrt(step_x * step_x + step_y * step_y + smoothing)
    flow_x = step_x / magnitude
    flow_y = step_y / magnitude
    spread = flow_x[1:, 1:] - flow_x[1:, :-1] + flow_y[1:, 1:] - flow_y[:-1, 1:]
    gradient = data_grad - tv_weight * spread
    return (residual, gradient)


lanes = 128
group = 32
num_groups = 4
bands = 4
band_size = 8
devices = 32
size = 1024
MESH = pl.DeviceIdType.MESH


def split_table(values):
    high = values.astype(jnp.bfloat16)
    return high, (values - high.astype(np.float64)).astype(jnp.bfloat16)


def tables():
    spot = np.arange(size)
    owner, column = (spot // group, spot % group)
    pixel = (owner % band_size) * lanes + (owner // band_size) * group + column
    frequency = (size // radix) * (spot % radix) + spot // radix
    angle = (frequency[:, None] * spot[None, :] % size) * (2.0 * np.pi / size)
    parts = np.stack([np.cos(angle), -np.sin(angle)]).reshape(2, devices, group, size)
    along_y = parts.transpose(1, 0, 2, 3).reshape(2 * size, size)
    angle = (pixel[:, None] * frequency[None, :] % size) * (2.0 * np.pi / size)
    cos_high, cos_low = split_table(np.cos(angle))
    sin_high, sin_low = split_table(np.sin(angle))
    return (
        *split_table(along_y),
        cos_high,
        sin_high,
        cos_low,
        sin_low,
        *split_table(np.ascontiguousarray(along_y.T)),
        *(np.ascontiguousarray(part.T) for part in (cos_high, sin_high, cos_low, sin_low)),
    )


def split(values):
    high = values.astype(jnp.bfloat16)
    return high, (values - high.astype(jnp.float32)).astype(jnp.bfloat16)


def mul(left, right):
    return jnp.dot(left, right, preferred_element_type=jnp.float32)


def cut(values, index):
    return values[:, index * group : (index + 1) * group]


def lane_groups(rows):
    return lax.broadcasted_iota(jnp.int32, (rows, lanes), 1) // group


def pick_groups(pieces):
    where = lane_groups(pieces[0].shape[0])
    out = pieces[0]
    for index in range(1, num_groups):
        out = jnp.where(where == index, pieces[index], out)
    return out


def fold(values):
    values = values + pltpu.roll(values, 64, 1)
    return values + pltpu.roll(values, 32, 1)


def encode(real, imag):
    largest = jnp.max(jnp.maximum(jnp.abs(real), jnp.abs(imag)), axis=0, keepdims=True)
    level = jnp.ceil(jnp.log2(jnp.maximum(largest, 1e-30)) * 256.0 + 0.01)
    factor = 32760.0 * jnp.exp2(level * (-1.0 / 256.0))
    high = jnp.floor(real * factor + 0.5).astype(jnp.int32)
    low = jnp.floor(imag * factor + 0.5).astype(jnp.int32)
    return high * 65536 + (low + 32768), level.astype(jnp.int32)


def decode(packed, level):
    factor = jnp.exp2(level.astype(jnp.float32) * (1.0 / 256.0)) * (1.0 / 32760.0)
    real = (packed >> 16).astype(jnp.float32) * factor
    imag = ((packed & 65535) - 32768).astype(jnp.float32) * factor
    return real, imag


def pull(total, sky, left, right, below, above, below_left, above_right):
    rows = sky.shape[0]
    lane = lax.broadcasted_iota(jnp.int32, sky.shape, 1)
    row = lax.broadcasted_iota(jnp.int32, sky.shape, 0)

    def flows(step_x, step_y):
        magnitude = jnp.sqrt(step_x * step_x + step_y * step_y + smoothing)
        return step_x / magnitude, step_y / magnitude

    next_x = jnp.where(lane == lanes - 1, right, pltpu.roll(sky, lanes - 1, 1))
    next_y = jnp.where(row == rows - 1, below, pltpu.roll(sky, rows - 1, 0))
    flow_x, flow_y = flows(next_x - sky, next_y - sky)
    left_next = jnp.where(row == rows - 1, below_left, pltpu.roll(left, rows - 1, 0))
    side_x, _ = flows(sky - left, left_next - left)
    side_x = side_x[:, 0:1]
    above_next = jnp.where(lane[0:8] == lanes - 1, above_right, pltpu.roll(above, lanes - 1, 1))
    _, top_y = flows(above_next - above, sky[0:1] - above)
    before_x = jnp.where(lane == 0, side_x, pltpu.roll(flow_x, 1, 1))
    before_y = jnp.where(row == 0, top_y[7:8], pltpu.roll(flow_y, 1, 0))
    total[...] = flow_x - before_x + flow_y - before_y


def kernel(
    sky, seen, noise, basis, lists, counts,
    trans_hbm, fyh_hbm, fyl_hbm, cxh_hbm, sxh_hbm, cxl_hbm, sxl_hbm, gh_hbm, gl_hbm,
    txh_hbm, uxh_hbm, txl_hbm, uxl_hbm,
    res_out, grad_out,
    trans, fyh, fyl, cxh, sxh, cxl, sxl, gh, gl, txh, uxh, txl, uxl,
    sky_s, sky_r, seen_s, seen_r, noise_s, noise_r, tile_s, tile_r,
    two_s, two_r, three_s, three_r, four_s, four_r, five_s, five_r,
    res_s, res_r, grad_s, grad_r,
    halo_left, halo_right, halo_below, halo_above, halo_bl, halo_ar,
    weights, fields, wide, narrow, tall, spread, spectra, pulled,
    load_sem, send_sem, recv_sem,
):
    my_y, my_x = (lax.axis_index("sy"), lax.axis_index("sx"))
    me = my_y * band_size + my_x
    barrier = pltpu.get_barrier_semaphore()

    def plane_at(step):
        return lax.rem(my_y // 2 + step // 2, 2) * 2 + lax.rem(my_y + step, 2)

    def greet(step, carry):
        other = lax.rem(me + step, devices)
        pl.semaphore_signal(
            barrier, inc=1, device_id=(other // band_size, lax.rem(other, band_size)),
            device_id_type=MESH,
        )
        return carry

    lax.fori_loop(1, devices, greet, 0)
    loads = []
    pairs = (
        (fyh_hbm, fyh), (fyl_hbm, fyl), (cxh_hbm, cxh), (sxh_hbm, sxh), (cxl_hbm, cxl),
        (sxl_hbm, sxl), (trans_hbm, trans), (txh_hbm, txh), (uxh_hbm, uxh), (txl_hbm, txl),
        (uxl_hbm, uxl), (gh_hbm, gh), (gl_hbm, gl),
    )
    for index, (source, target) in enumerate(pairs):
        loads.append(pltpu.make_async_copy(source, target, load_sem.at[index]))
        loads[-1].start()

    def send(source, target, phase, where, arrival=None):
        arrival = phase if arrival is None else arrival
        pltpu.make_async_remote_copy(
            src_ref=source, dst_ref=target, send_sem=send_sem.at[phase],
            recv_sem=recv_sem.at[arrival], device_id=where, device_id_type=MESH,
        ).start()

    def total_of(buffer, phase, count=None):
        part = buffer.at[pl.ds(0, buffer.shape[0] - 1 if count is None else count)]
        return pltpu.make_async_remote_copy(
            src_ref=part, dst_ref=part, send_sem=send_sem.at[phase],
            recv_sem=recv_sem.at[phase], device_id=(lax.rem(my_y + 1, bands), my_x),
            device_id_type=MESH,
        )

    def arrived(buffer, first, plane):
        @pl.when(plane != my_y)
        def _():
            total_of(buffer, first + plane, band_size).wait_recv()

        @pl.when(plane == my_y)
        def _():
            total_of(buffer, first + plane, band_size - 1).wait_recv()

    def to_all(source, target, phase, other, arrival=None):
        @pl.when(other != me)
        def _():
            send(
                source.at[other], target.at[me], phase,
                (other // band_size, lax.rem(other, band_size)), arrival,
            )

        @pl.when(other == me)
        def _():
            target[me] = source[me]

    def to_band(source, target, phase, other):
        @pl.when(other != my_y)
        def _():
            send(source.at[other], target.at[my_y], phase, (other, my_x))

        @pl.when(other == my_y)
        def _():
            target[my_y] = source[my_y]

    def pack(block, other):
        return jnp.concatenate(
            [cut(block[g * 64 : (g + 1) * 64], other) for g in range(num_groups)], axis=1
        )

    row = lax.broadcasted_iota(jnp.int32, (8, lanes), 0)
    mask = jnp.where(row % 4 < jnp.where(row < 4, counts[0, 0], counts[1, 0]), 1.0, 0.0)
    slot_lane = lane_groups(64) % 2
    for other in range(bands):
        sky_s[other, 0:64] = pack(sky[...], other)
        sky_s[other, 64:72] = mask
    pl.semaphore_wait(barrier, devices - 1)
    for step in range(bands):
        to_band(sky_s, sky_r, 0, lax.rem(my_y + 1 + step, bands))

    for other in range(bands):
        packs = []
        for t in range(4):
            part = cut(basis[t].astype(jnp.float32), other)
            packs.append(
                jnp.concatenate([part[0:64], part[0:64], part[64:128], part[64:128]], axis=1)
            )

        def choose(column, carry):
            first, second, seen_before = (-1, -1, 0)
            for e in range(8):
                local = lists[my_y * 2 + e // 4, column, e % 4] - me * 4
                hit = (local >= 0) & (local < 4)
                first = jnp.where(hit & (seen_before == 0), local, first)
                second = jnp.where(hit & (seen_before == 1), local, second)
                seen_before = seen_before + jnp.where(hit, 1, 0)
            wanted = jnp.where(slot_lane == 0, first, second)
            acc = jnp.where(wanted == 0, packs[0], 0.0)
            for t in range(1, 4):
                acc = jnp.where(wanted == t, packs[t], acc)
            tile_s[other * band_size + column] = acc.astype(jnp.bfloat16)
            return carry

        lax.fori_loop(0, band_size, choose, 0)

    def send_tiles(step, carry):
        plane = plane_at(3 - step // band_size)
        to_all(tile_s, tile_r, 1, plane * band_size + lax.rem(my_x + step, band_size))
        return carry

    lax.fori_loop(0, devices, send_tiles, 0)

    for other in range(bands):
        seen_s[other] = pack(seen[...], other)
        noise_s[other] = pack(noise[...], other)
    for step in range(bands):
        to_band(seen_s, seen_r, 2, lax.rem(my_y + 1 + step, bands))
        to_band(noise_s, noise_r, 3, lax.rem(my_y + 1 + step, bands))
    up, down = (lax.rem(my_y + bands - 1, bands), lax.rem(my_y + 1, bands))
    west, east = (lax.rem(my_x + band_size - 1, band_size), lax.rem(my_x + 1, band_size))
    first, last = (sky.at[pl.ds(0, 8)], sky.at[pl.ds(248, 8)])
    halos = (
        (sky_s.at[0, pl.ds(0, 64)], halo_right, (my_y, west)),
        (sky_s.at[bands - 1, pl.ds(0, 64)], halo_left, (my_y, east)),
        (first, halo_below, (up, my_x)),
        (first, halo_bl, (up, east)),
        (last, halo_above, (down, my_x)),
        (last, halo_ar, (down, west)),
    )
    for index, (source, target, where) in enumerate(halos):
        send(source, target, 9 + index, where)

    total_of(sky_r, 0).wait_recv()
    total_of(tile_r, 1).wait_recv()

    def weigh(band, carry):
        parts = []
        tiles = [tile_r[band * band_size + h].astype(jnp.float32) for h in range(band_size)]
        holders = [
            lists[band * 2 + e // 4, my_x, e % 4] // 4 - band * band_size for e in range(8)
        ]
        for e in range(8):
            slot = 0
            for earlier in range(e):
                slot = slot + jnp.where(holders[earlier] == holders[e], 1, 0)
            place = holders[e] * 2 + slot
            acc = jnp.zeros((64, lanes), jnp.float32)
            for h in range(band_size):
                acc = jnp.where(slot_lane + 2 * h == place, tiles[h], acc)
            acc = (acc + pltpu.roll(acc, 96, 1)) * sky_r[band, 64 + e : 65 + e]
            parts.append(acc)
        for g in range(num_groups):
            down_tile, half = (g // 2, g % 2)
            block = jnp.concatenate(
                [cut(parts[down_tile * 4 + k], 2 * half) for k in range(4)], axis=1
            )
            rows = pl.ds(pl.multiple_of(band * 256 + g * 64, 64), 64)
            weights[rows] = block
            high, low = split(
                block * jnp.concatenate([cut(sky_r[band, 0:64], g)] * num_groups, axis=1)
            )
            fields[rows, 0:128] = high
            fields[rows, 128:256] = low
        return carry

    lax.fori_loop(0, bands, weigh, 0)
    loads[0].wait()
    loads[1].wait()

    def along_y(step):
        part = plane_at(3 - step // 2) * 2 + lax.rem(step + my_x, 2)
        rows = pl.ds(pl.multiple_of(part * 256, 256), 256)
        both = mul(fyh[rows], fields[...])
        return part, both[:, 0:128] + both[:, 128:256] + mul(fyl[rows], fields[:, 0:128])

    def forward_y(step, carry):
        part, out = along_y(step)
        for j in range(4):
            other = part * 4 + j
            packed, level = encode(out[j * 64 : j * 64 + 32], out[j * 64 + 32 : j * 64 + 64])
            two_s[other, 0:32] = packed
            two_s[other, 32:40] = jnp.broadcast_to(level, (8, lanes))
        for j in range(4):
            to_all(two_s, two_r, 4, part * 4 + lax.rem(my_x + j, 4), 16 + my_y)
        return carry

    lax.fori_loop(0, 8, forward_y, 0)

    for index, (source, target, where) in enumerate(halos):
        pltpu.make_async_remote_copy(
            src_ref=source, dst_ref=target, send_sem=send_sem.at[9 + index],
            recv_sem=recv_sem.at[9 + index], device_id=where, device_id_type=MESH,
        ).wait()

    def side(buffer, lane):
        return jnp.concatenate(
            [
                buffer[:, g * group + lane : g * group + lane + 1] + jnp.zeros((64, lanes))
                for g in range(num_groups)
            ],
            axis=0,
        )

    pull(
        spread, sky[...], side(halo_left, group - 1), side(halo_right, 0), halo_below[0:1],
        halo_above[...], halo_bl[0:1, 127:128], halo_ar[7:8, 0:1],
    )

    for index in range(2, 7):
        loads[index].wait()

    def gather_two(g):
        at = pl.ds(pl.multiple_of(g * 128, 128), 128)
        parts = [decode(two_r[4 * g + j, 0:32], two_r[4 * g + j, 32:33]) for j in range(4)]
        for c in range(2):
            blocks = [part[c] for part in parts]
            for k in range(4):
                high, low = split(jnp.concatenate([cut(block, k) for block in blocks], axis=1))
                row = c * 128 + k * 32
                wide[row : row + 32, at] = high
                wide[256 + row : 288 + row, at] = low

    def along_x(buffer, half, at, inner):
        cos_part = mul(buffer[:, inner], cxh[inner, at])
        sin_part = mul(buffer[:, inner], sxh[inner, at])
        cos_part = cos_part[0:half] + cos_part[half:] + mul(buffer[0:half, inner], cxl[inner, at])
        sin_part = sin_part[0:half] + sin_part[half:] + mul(buffer[0:half, inner], sxl[inner, at])
        q = half // 2
        return cos_part[0:q] + sin_part[q:half], cos_part[q:half] - sin_part[0:q]

    spectra[...] = jnp.zeros_like(spectra)

    def add_plane(step, carry):
        plane = plane_at(step)
        arrived(two_r, 16, plane)
        gather_two(plane * 2)
        gather_two(plane * 2 + 1)
        inner = pl.ds(pl.multiple_of(plane * 256, 256), 256)
        for n in range(4):
            at = slice(n * 256, (n + 1) * 256)
            real, imag = along_x(wide, 256, at, inner)
            spectra[0, :, at] += real
            spectra[1, :, at] += imag
        return carry

    lax.fori_loop(0, bands, add_plane, 0)

    def back_x(buffer, half, rows):
        cos_part = mul(buffer[...], txh[:, rows])
        sin_part = mul(buffer[...], uxh[:, rows])
        cos_part = cos_part[0:half] + cos_part[half:] + mul(buffer[0:half], txl[:, rows])
        sin_part = sin_part[0:half] + sin_part[half:] + mul(buffer[0:half], uxl[:, rows])
        q = half // 2
        return cos_part[0:q] - sin_part[q:half], cos_part[q:half] + sin_part[0:q]

    def model(step, carry):
        at = pl.ds(pl.multiple_of(step * 256, 256), 256)
        real, imag = (spectra[0, :, at], spectra[1, :, at])
        sum_real, sum_imag = (0.0, 0.0)
        for k in range(4):
            rows = slice(k * 32, (k + 1) * 32)
            trans_real, trans_imag = (trans[k, 0, :, at], trans[k, 1, :, at])
            sum_real = sum_real + real[rows] * trans_real - imag[rows] * trans_imag
            sum_imag = sum_imag + real[rows] * trans_imag + imag[rows] * trans_real
        for c, part in enumerate((sum_real, sum_imag)):
            high, low = split(part)
            narrow[c * 32 : (c + 1) * 32, at] = high
            narrow[64 + c * 32 : 96 + c * 32, at] = low
        return carry

    lax.fori_loop(0, 4, model, 0)

    for index in range(7, 11):
        loads[index].wait()

    def back_three(step, carry):
        part = plane_at(3 - step)
        rows = pl.ds(pl.multiple_of(part * 256, 256), 256)
        real, imag = back_x(narrow, 64, rows)
        for j in range(8):
            other = part * 8 + j
            three_s[other] = jnp.concatenate(
                [cut(real[0:16], j), cut(imag[0:16], j), cut(real[16:32], j), cut(imag[16:32], j)],
                axis=1,
            )
        for j in range(8):
            to_all(three_s, three_r, 5, part * 8 + lax.rem(my_x + j, 8))
        return carry

    lax.fori_loop(0, 4, back_three, 0)
    loads[11].wait()
    loads[12].wait()
    total_of(seen_r, 2).wait_recv()
    total_of(noise_r, 3).wait_recv()
    total_of(three_r, 5).wait_recv()

    def spread_three(source, carry):
        block = three_r[source]
        where = lane_groups(16)
        for c in range(2):
            for h in range(2):
                high, low = split(jnp.where(where == h * 2 + c, block, 0.0))
                rows = pl.ds(pl.multiple_of(source * 64 + c * 32 + h * 16, 16), 16)
                tall[rows, 0:128] = high
                tall[rows, 128:256] = low
        return carry

    lax.fori_loop(0, devices, spread_three, 0)
    normalizer = 1.0 / (size * size)

    def back_y(rows):
        both = mul(gh[rows], tall[...])
        out = both[:, 0:128] + both[:, 128:256] + mul(gl[rows], tall[:, 0:128])
        return out * normalizer

    def residual(step, carry):
        band = plane_at(3 - step)
        rows = pl.ds(pl.multiple_of(band * 256, 256), 256)
        out = fold(back_y(rows))
        blurred = pick_groups([out[g * 64 : (g + 1) * 64] for g in range(num_groups)])
        left_over = noise_r[band] * (blurred - seen_r[band])
        res_s[band] = left_over
        for g in range(num_groups):
            high, low = split(jnp.concatenate([cut(left_over, g)] * num_groups, axis=1))
            rows = pl.ds(pl.multiple_of(band * 256 + g * 64, 64), 64)
            fields[rows, 0:128] = high
            fields[rows, 128:256] = low
        return carry

    lax.fori_loop(0, bands, residual, 0)

    def forward_four(step, carry):
        part, out = along_y(step)
        for j in range(4):
            other = part * 4 + j
            pieces = []
            for h in range(2):
                for c in range(2):
                    row = j * 64 + c * 32 + h * 16
                    pieces.append(out[row : row + 16])
            four_s[other] = pick_groups(pieces)
        for j in range(4):
            to_all(four_s, four_r, 6, part * 4 + lax.rem(my_x + j, 4))
        return carry

    lax.fori_loop(0, 8, forward_four, 0)
    for other in range(bands):
        to_band(res_s, res_r, 8, other)
    total_of(four_r, 6).wait_recv()

    def gather_four(g, carry):
        at = pl.ds(pl.multiple_of(g * 128, 128), 128)
        blocks = [four_r[4 * g + j] for j in range(4)]
        for c in range(2):
            for h in range(2):
                high, low = split(
                    jnp.concatenate([cut(block, h * 2 + c) for block in blocks], axis=1)
                )
                row = c * 32 + h * 16
                narrow[row : row + 16, at] = high
                narrow[64 + row : 80 + row, at] = low
        return carry

    lax.fori_loop(0, 8, gather_four, 0)

    def adjoint(step, carry):
        at = pl.ds(pl.multiple_of(step * 256, 256), 256)
        real, imag = along_x(narrow, 64, at, slice(None))
        for k in range(4):
            trans_real, trans_imag = (trans[k, 0, :, at], trans[k, 1, :, at])
            both = (real * trans_real + imag * trans_imag, imag * trans_real - real * trans_imag)
            for c in range(2):
                high, low = split(both[c])
                row = c * 128 + k * 32
                wide[row : row + 32, at] = high
                wide[256 + row : 288 + row, at] = low
        return carry

    lax.fori_loop(0, 4, adjoint, 0)

    def back_five(step, carry):
        part = plane_at(3 - step)
        rows = pl.ds(pl.multiple_of(part * 256, 256), 256)
        both = back_x(wide, 256, rows)
        for j in range(8):
            other = part * 8 + j
            real, imag = [
                jnp.concatenate([cut(part[k * 32 : (k + 1) * 32], j) for k in range(4)], axis=1)
                for part in both
            ]
            packed, level = encode(real, imag)
            five_s[other, 0:32] = packed
            five_s[other, 32:40] = jnp.broadcast_to(level, (8, lanes))
        for j in range(8):
            to_all(five_s, five_r, 7, part * 8 + lax.rem(my_x + j, 8), 20 + my_y)
        return carry

    lax.fori_loop(0, 4, back_five, 0)
    pulled[...] = jnp.zeros_like(pulled)

    def split_five(source, carry):
        parts = decode(five_r[source, 0:32], five_r[source, 32:33])
        for c in range(2):
            high, low = split(parts[c])
            rows = pl.ds(pl.multiple_of(source * 64 + c * 32, 32), 32)
            tall[rows, 0:128] = high
            tall[rows, 128:256] = low
        return carry

    def add_five(step, carry):
        plane = plane_at(step)
        arrived(five_r, 20, plane)
        lax.fori_loop(plane * band_size, (plane + 1) * band_size, split_five, 0)
        inner = pl.ds(pl.multiple_of(plane * 512, 512), 512)
        for band in range(bands):
            rows = slice(band * 256, (band + 1) * 256)
            both = mul(gh[rows, inner], tall[inner])
            both = both[:, 0:128] + both[:, 128:256] + mul(gl[rows, inner], tall[inner, 0:128])
            pulled[rows] += both
        return carry

    lax.fori_loop(0, bands, add_five, 0)

    def finish(step, carry):
        band = plane_at(3 - step)
        rows = pl.ds(pl.multiple_of(band * 256, 256), 256)
        out = fold(pulled[rows] * weights[rows] * normalizer)
        grad_s[band] = pick_groups([out[g * 64 : (g + 1) * 64] for g in range(num_groups)])
        to_band(grad_s, grad_r, 15, band)
        return carry

    lax.fori_loop(0, bands, finish, 0)
    total_of(res_r, 8).wait_recv()
    total_of(grad_r, 15).wait_recv()
    for g in range(num_groups):
        rows = slice(g * 64, (g + 1) * 64)
        res_out[rows] = jnp.concatenate([cut(res_r[band], g) for band in range(bands)], axis=1)
        grad_out[rows] = (
            jnp.concatenate([cut(grad_r[band], g) for band in range(bands)], axis=1)
            - tv_weight * spread[rows]
        )
    for buffer, phase in (
        (sky_s, 0), (tile_s, 1), (seen_s, 2), (noise_s, 3), (two_s, 4), (three_s, 5),
        (four_s, 6), (five_s, 7), (res_s, 8), (grad_s, 15),
    ):
        total_of(buffer, phase).wait_send()


def on_device(sky_image, observed, noise_weight, basis_tiles, intersection, counts, transfer):
    pool, tile_side = (basis_tiles.shape[0], basis_tiles.shape[1])
    shape = (lax.axis_size("sy"), lax.axis_size("sx"), *sky_image.shape, pool, tile_side)
    if shape + intersection.shape[2:] != (bands, band_size, 256, lanes, 4, lanes, 4):
        return generic_device(
            sky_image, observed, noise_weight, basis_tiles, intersection, counts, transfer
        )
    constants = tables()
    f32, bf16 = (jnp.float32, jnp.bfloat16)
    scalars = pl.BlockSpec(memory_space=pltpu.SMEM)

    def double(*dims, kind=f32):
        return [pltpu.VMEM(dims, kind)] * 2

    scratch = [
        pltpu.VMEM(transfer.shape, f32),
        *[pltpu.VMEM(table.shape, bf16) for table in constants],
        *double(bands, 72, lanes),
        *double(bands, 64, lanes),
        *double(bands, 64, lanes),
        *double(devices, 64, lanes, kind=bf16),
        *double(devices, 40, lanes, kind=jnp.int32),
        *double(devices, 16, lanes),
        *double(devices, 16, lanes),
        *double(devices, 40, lanes, kind=jnp.int32),
        *double(bands, 64, lanes),
        *double(bands, 64, lanes),
        *double(64, lanes),
        *double(8, lanes),
        *double(8, lanes),
        pltpu.VMEM((size, lanes), f32),
        pltpu.VMEM((size, 2 * lanes), bf16),
        pltpu.VMEM((512, size), bf16),
        pltpu.VMEM((128, size), bf16),
        pltpu.VMEM((2 * size, 2 * lanes), bf16),
        pltpu.VMEM((256, lanes), f32),
        pltpu.VMEM((2, lanes, size), f32),
        pltpu.VMEM((size, lanes), f32),
        pltpu.SemaphoreType.DMA((13,)),
        pltpu.SemaphoreType.DMA((16,)),
        pltpu.SemaphoreType.DMA((24,)),
    ]
    in_vmem = pl.BlockSpec(memory_space=pltpu.VMEM)
    outside = pl.BlockSpec(memory_space=pl.ANY)
    return pl.pallas_call(
        kernel,
        out_shape=[jax.ShapeDtypeStruct(sky_image.shape, f32)] * 2,
        in_specs=[in_vmem] * 4 + [scalars] * 2 + [outside] * 13,
        out_specs=[in_vmem] * 2,
        scratch_shapes=scratch,
        compiler_params=pltpu.CompilerParams(
            collective_id=0, has_side_effects=True, vmem_limit_bytes=56 * 1024 * 1024
        ),
        cost_estimate=pl.CostEstimate(
            flops=10_000_000_000, bytes_accessed=30_000_000, transcendentals=0
        ),
    )(
        sky_image, observed, noise_weight, basis_tiles, intersection, counts, transfer, *(jnp.asarray(table) for table in constants),
    )


def solution(mesh):
    placed = (
        P("sy", "sx"),
        P("sy", "sx"),
        P("sy", "sx"),
        P(("sy", "sx"), None, None),
        P(),
        P("sy", "sx"),
        P(None, None, ("sy", "sx"), None),
    )
    return jax.shard_map(
        on_device,
        mesh=mesh,
        in_specs=placed,
        out_specs=(P("sy", "sx"), P("sy", "sx")),
        check_vma=False,
    )
```
